128 devices in a mesh: grp: 4 (over z), ep: 32 (over x, y, core).
Axes of the slice: x: 4, y: 4, z: 4, core: 2. Of those that a mesh axis runs over, the one named last changes fastest.
Arguments:
- attention: bfloat16 [16384, 1024], P(('grp', 'ep')), may hold values from -6 to 6
- residual: bfloat16 [16384, 1024], P(('grp', 'ep')), may hold values from -6 to 6
- out_proj: bfloat16 [1024, 1024], P(None, 'grp'), may hold values from -0.1875 to 0.1875
- pre_gain: float32 [1024], replicated, may hold values from 0.25 to 1.75
- post_gain: float32 [1024], replicated, may hold values from 0.25 to 1.75
- slot_gate_up: bfloat16 [32, 1024, 1024], P('ep'), may hold values from -0.1875 to 0.1875
- slot_down: bfloat16 [32, 512, 1024], P('ep'), may hold values from -0.25 to 0.25
- expert_ids: int32 [16384, 8], P(('grp', 'ep')), may hold values from 0 to 31, all different within a row
- copy_choice: int32 [16384, 8], P(('grp', 'ep')), may hold values from 0 to 3
- placement: int32 [32], replicated, may hold values from 0 to 31, each once
- request_age: int32 [16384], P(('grp', 'ep')), may hold values from 0 to 1048575
- decode_flag: int32 [16384], P(('grp', 'ep')), may hold values 0 or 1
- capacity: int32 [4, 32], replicated, may hold values from 4 to 8, as said below
- route_weight: float32 [16384, 8], P(('grp', 'ep')), may hold values from 0.05 to 1
Outputs:
- layer_out: bfloat16 [16384, 1024], P(('grp', 'ep'))
The draws below stay inside these ranges and needn't reach their ends.
Inputs may be any that keep to these rules, and one draw needn't show every extreme that they name: At least one block has capacity 8. `expert_ids`: each row names 8 different experts. `placement`: each slot holds a different expert.
All inputs are finite; a program needn't handle non-finite values. No bound on the sum of `decode_flag` on one device may be relied on, other than what follows from the above.
Results may differ from the reference program's by a relative error of at most 0.01.
Values may be sent and summed in bfloat16 or wider, within the bound.
A program may use at most 64 MiB of HBM per device.

```python
import math
import jax
import jax.numpy as jnp
from jax import lax

D = 1024
FF = 512
TOPK = 8
ROWS_DEV = 128
EXPERTS = 32
ROWS = 16384
CAP = 8
N_GRP = 4
N_EP = 32


def draw_capacity(key, part):
    first, second = jax.random.split(key)
    lowest = max(1, CAP // 2)
    levels = jax.random.randint(first, (N_GRP * N_EP,), lowest, CAP + 1)
    chosen = jax.random.randint(second, (), 0, N_GRP * N_EP)
    levels = levels.at[chosen].set(CAP)
    return levels.reshape(N_GRP, N_EP).astype(jnp.int32)


def draw_request_age(key, part):
    first, second = jax.random.split(jax.random.fold_in(key, 17))
    ages = jax.random.randint(first, (ROWS,), 0, 64)
    chosen = jax.random.randint(second, (), 0, ROWS)
    ages = ages.at[chosen].set(1048575)
    ages = ages.at[(chosen + 1) % ROWS].set(0)
    return ages.astype(jnp.int32)


def with_ends(values, own_key, smallest, largest):
    spot = [jax.random.randint(jax.random.fold_in(own_key, axis), (), 0, length) for axis, length in enumerate(values.shape)]
    main_axis = values.shape.index(max(values.shape))
    neighbour = spot[:main_axis] + [(spot[main_axis] + 1) % values.shape[main_axis]] + spot[main_axis + 1:]
    return values.at[tuple(spot)].set(smallest).at[tuple(neighbour)].set(largest)


def block_levels(rng, extent, shards, smallest, largest):
    def one(dim, shards_of):
        steps = jax.random.uniform(jax.random.fold_in(jax.random.fold_in(rng, 6), dim), (shards_of,), jnp.float32, smallest / len(shards), largest / len(shards))
        return jnp.repeat(jnp.exp(steps), extent[dim] // shards_of).reshape((-1,) + (1,) * (len(extent) - dim - 1))

    loudness = one(*shards[0])
    for cut in shards[1:]:
        loudness = loudness * one(*cut)
    return loudness


def distinct(rng, rows, amount, top, lift):
    ranking = jax.random.permutation(jax.random.fold_in(rng, 1), amount)
    favour = ranking
    for power in range(3):
        favour = favour * favour // amount
    favour = favour * lift // amount
    chance = jax.random.randint(jax.random.fold_in(rng, 2), (rows, amount), 0, 4096) + favour
    fixed_rows = jax.random.permutation(jax.random.fold_in(rng, 3), rows)[jnp.arange(amount) % rows]
    chance = jnp.where(jnp.arange(rows)[:, None] == fixed_rows[None, :], 1 << 14, chance)
    score = chance * amount + jnp.arange(amount)
    return lax.top_k(score.astype(jnp.int32), top)[1].astype(jnp.int32)


def gaussian(stream_key, shape, width, reach, cuts=(), kind=jnp.bfloat16):
    entries = width * jax.random.normal(stream_key, shape, jnp.float32)
    if cuts:
        entries = entries * block_levels(stream_key, shape, cuts, -0.22, 0.18)
    return jnp.clip(entries, -reach, reach).astype(kind)


def setup_inputs(seed: int = 0) -> dict:
    keys = jax.random.split(jax.random.key(seed), 15)
    return {
        "attention": gaussian(keys[0], (ROWS, D), 1.0, 6.0, ((0, 128),)),
        "residual": gaussian(keys[1], (ROWS, D), 1.0, 6.0, ((0, 128),)),
        "out_proj": gaussian(keys[2], (D, D), D ** -0.5, 0.1875, ((1, 4),)),
        "pre_gain": jnp.clip(1.0 + 0.15 * jax.random.normal(keys[3], (D,), jnp.float32), 0.25, 1.75),
        "post_gain": jnp.clip(1.0 + 0.15 * jax.random.normal(keys[4], (D,), jnp.float32), 0.25, 1.75),
        "slot_gate_up": gaussian(keys[5], (N_EP, D, 2 * FF), D ** -0.5, 0.1875, ((0, 32),)),
        "slot_down": gaussian(keys[6], (N_EP, FF, D), FF ** -0.5, 0.25, ((0, 32),)),
        "expert_ids": distinct(keys[7], ROWS, EXPERTS, TOPK, 4096),
        "copy_choice": with_ends(jax.random.randint(keys[8], (ROWS, TOPK), 0, N_GRP), jax.random.fold_in(keys[8], 1), 0, N_GRP - 1).astype(jnp.int32),
        "placement": jax.random.permutation(keys[9], N_EP).astype(jnp.int32),
        "request_age": draw_request_age(jax.random.fold_in(keys[14], 71), 0),
        "decode_flag": with_ends((jax.random.randint(keys[11], (ROWS,), 0, 3) < 1).astype(jnp.int32), jax.random.fold_in(keys[11], 1), 0, 1),
        "capacity": draw_capacity(jax.random.fold_in(keys[14], 71), 0),
        "route_weight": jnp.clip(jnp.exp(math.log(1.0) - 2.9957323 * jax.random.uniform(keys[13], (ROWS, TOPK), jnp.float32) ** block_levels(keys[13], (ROWS, TOPK), ((0, 128),), -0.2, 0.2)), 0.05, 1.0),
    }


def rms_scale(values, gain):
    meansq = lax.optimization_barrier(jnp.mean(values * values, axis=-1, keepdims=True))
    return values * lax.rsqrt(meansq + 1e-06) * gain

def reference(attention, residual, out_proj, pre_gain, post_gain, slot_gate_up, slot_down, expert_ids, copy_choice, placement, request_age, decode_flag, capacity, route_weight):
    devices_all = N_GRP * N_EP
    attn_proj = jnp.dot(attention, out_proj, preferred_element_type=jnp.float32)
    hidden_state = (residual.astype(jnp.float32) + attn_proj).astype(jnp.bfloat16)
    normed = rms_scale(hidden_state.astype(jnp.float32), pre_gain).astype(jnp.bfloat16)
    slot_table = jnp.arange(N_EP, dtype=jnp.int32)
    matches = (placement[None, :] == jnp.arange(EXPERTS, dtype=jnp.int32)[:, None]).astype(jnp.int32)
    slot_of = lax.optimization_barrier(jnp.sum(slot_table[None, :] * matches, axis=1)).astype(jnp.int32)
    target = (copy_choice * N_EP + slot_of[expert_ids]).astype(jnp.int32)
    priority = (decode_flag * 1048576 + request_age).astype(jnp.int32)

    def block_position(pieces):
        target_block, priority_block = pieces
        hits = lax.optimization_barrier(jnp.sum((target_block[:, :, None] == jnp.arange(devices_all, dtype=jnp.int32)[None, None, :]).astype(jnp.float32), axis=1))
        order = jnp.arange(ROWS_DEV, dtype=jnp.int32)
        ahead_mask = (priority_block[None, :] > priority_block[:, None]) | (priority_block[None, :] == priority_block[:, None]) & (order[None, :] < order[:, None])
        counts = jnp.dot(ahead_mask.astype(jnp.float32), hits, precision=lax.Precision.HIGHEST)
        return jnp.take_along_axis(counts, target_block, axis=1).astype(jnp.int32)
    position = lax.map(block_position, (target.reshape(devices_all, ROWS_DEV, TOPK), priority.reshape(devices_all, ROWS_DEV)))
    position = position.reshape(ROWS, TOPK)
    accepted = position < capacity.reshape(-1)[target]
    source = (jnp.arange(ROWS, dtype=jnp.int32) // ROWS_DEV)[:, None]
    total_slots = devices_all * devices_all * CAP
    index = jnp.where(accepted, target * (devices_all * CAP) + source * CAP + position, total_slots).astype(jnp.int32)
    spread_rows = jnp.broadcast_to(normed[:, None, :], (ROWS, TOPK, D)).reshape(ROWS * TOPK, D)
    buffer = jnp.zeros((total_slots, D), jnp.bfloat16).at[index.reshape(-1)].set(spread_rows, mode='drop')

    def apply_expert(pieces):
        slot_rows, slot = pieces
        gate_up = jnp.dot(slot_rows, slot_gate_up[slot], preferred_element_type=jnp.float32)
        expert_hidden = (jax.nn.silu(gate_up[:, :FF]) * gate_up[:, FF:]).astype(jnp.bfloat16)
        return jnp.dot(expert_hidden, slot_down[slot], preferred_element_type=jnp.float32).astype(jnp.bfloat16)
    slots = jnp.arange(devices_all, dtype=jnp.int32) % N_EP
    results = lax.map(apply_expert, (buffer.reshape(devices_all, devices_all * CAP, D), slots)).reshape(total_slots, D)
    expert_out = results[jnp.minimum(index, total_slots - 1)]
    weights_kept = jnp.where(accepted, route_weight, jnp.float32(0.0))
    mixture = jnp.einsum('rk,rkd->rd', weights_kept, expert_out.astype(jnp.float32))
    return rms_scale(hidden_state.astype(jnp.float32) + mixture, post_gain).astype(jnp.bfloat16)
```

```python
import functools

import jax
import jax.numpy as jnp
from jax import lax
from jax.experimental import pallas as pl
from jax.experimental.pallas import tpu as pltpu
from jax.sharding import PartitionSpec as P

MESH = pl.DeviceIdType.MESH
BF = jnp.bfloat16
F32 = jnp.float32
FAR = (2, 1, 3)
NEAR = (1, 3, 2)


def dot(a, b):
    return jnp.dot(a, b, preferred_element_type=F32)


def kernel(
    att_h, res_h, wo_h, pre_h, post_h, gu_h, dn_h, ids_h, cc_h, place_h, age_h, flag_h, cap_h, rw_h,
    out_ref,
    att, res, pre, post, gu, dn, ids, cc, place, age, flag, cap, rw,
    wfull, proj, hid, src1, s1, mw_src, mw_rcv, sel, comb_w, comp, rec, ob, comb, part_src, part_rcv,
    in_sem, w_s, w_r, f_s, f_r, m_s, m_r, a_s, a_r, d_s, d_r, e_s, e_r, p_s, p_r,
):
    z = lax.axis_index("grp")
    e = lax.axis_index("ep")
    x, y, c = e // 8, (e // 2) % 4, e % 2

    def at(dx, dy, dz, dc):
        return ((z + dz) % 4, (((x + dx) % 4) * 4 + (y + dy) % 4) * 2 + (c + dc) % 2)

    def along(half, d, dc):
        return at(d, 0, 0, dc) if half == 0 else at(0, d, 0, dc)

    bar = pltpu.get_barrier_semaphore()
    greet = [(0, 0, 1, 0), (0, 0, 2, 0), (0, 0, 3, 0), (0, 0, 0, 1)]
    for d in (1, 2, 3):
        for dc in (0, 1):
            greet += [(d, 0, 0, dc), (0, d, 0, dc)]
    for off in greet:
        pl.semaphore_signal(bar, inc=1, device_id=at(*off), device_id_type=MESH)

    loads = []
    for i, (src, dst) in enumerate(
        (
            (ids_h, ids), (cc_h, cc), (place_h, place), (age_h, age), (flag_h, flag), (cap_h, cap), (rw_h, rw),
            (att_h, att), (wo_h, wfull.at[0]), (res_h, res), (pre_h, pre), (post_h, post), (gu_h, gu), (dn_h, dn),
        )
    ):
        cp = pltpu.make_async_copy(src, dst, in_sem.at[i])
        cp.start()
        loads.append(cp)

    sends = []

    def remote(src, dst, ss, rs, dev):
        cp = pltpu.make_async_remote_copy(
            src_ref=src, dst_ref=dst, send_sem=ss, recv_sem=rs, device_id=dev, device_id_type=MESH
        )
        cp.start()
        sends.append(cp)
        return cp

    pl.semaphore_wait(bar, len(greet))
    w_cp = {}
    for d in NEAR:
        w_cp[d] = remote(wo_h.at[c], wfull.at[d, c], w_s.at[d - 1], w_r.at[d - 1], at(0, 0, d, 0))

    for cp in loads[:7]:
        cp.wait()
    row = lax.broadcasted_iota(jnp.int32, (128, 128), 0)
    lane = lax.broadcasted_iota(jnp.int32, (128, 128), 1)
    pr_row = (flag[...] * 1048576 + age[...]).astype(F32)
    pr_col = jnp.sum(jnp.where(row == lane, jnp.broadcast_to(pr_row, (128, 128)), 0.0), axis=1, keepdims=True)
    ahead = jnp.where((pr_col > pr_row) | ((pr_col == pr_row) & (row < lane)), 1.0, 0.0)
    t = lax.broadcasted_iota(jnp.int32, (128, 32), 0)
    slot_lane = lax.broadcasted_iota(jnp.int32, (128, 32), 1)
    copy_of = t % 4
    slot = (((x + t // 32) % 4) * 4 + (y + (t // 4) % 4) % 4) * 2 + (c + (t // 16) % 2) % 2
    here = slot_lane == slot
    expert = jnp.sum(jnp.where(here, place[...].astype(F32), 0.0), axis=1, keepdims=True)
    code_col = expert * 4.0 + copy_of[:, :1].astype(F32)
    capf = cap[...].astype(F32)
    cap_sel = jnp.zeros((128, 32), F32)
    for g in range(4):
        cap_sel = jnp.where(here & (copy_of == g), capf[g : g + 1, :], cap_sel)
    cap_col = jnp.sum(cap_sel, axis=1, keepdims=True)
    code = (ids[...] * 4 + cc[...]).astype(F32)
    hits = jnp.zeros((128, 128), F32)
    weight = jnp.zeros((128, 128), F32)
    for k in range(8):
        same = code_col == code[k : k + 1, :]
        hits = jnp.where(same, 1.0, hits)
        weight = jnp.where(same, rw[k : k + 1, :], weight)
    counts = dot(hits.astype(BF), ahead.astype(BF))
    place_in = jnp.where((hits > 0.5) & (counts < cap_col), counts, 99.0)
    mw = jnp.concatenate([place_in, weight], axis=1).astype(BF)
    pw = jnp.concatenate([place_in, weight], axis=1)
    for d in range(4):
        mw_src[0, d] = pw[d * 32 : d * 32 + 32].astype(BF)
        blocks = []
        for dc in range(2):
            for dx in range(4):
                lo = dx * 32 + dc * 16 + d * 4
                blocks.append(pw[lo : lo + 4])
        mw_src[1, d] = jnp.concatenate(blocks, axis=0).astype(BF)
    del mw
    m_cp = {}
    for d in NEAR:
        for h in (0, 1):
            m_cp[h, d] = remote(
                mw_src.at[h, d], mw_rcv.at[h, d - 1], m_s.at[h, d - 1], m_r.at[h, d - 1], along(h, d, 0)
            )

    grow = jnp.where(
        lax.broadcasted_iota(jnp.int32, (256, 32), 0) // 8 == lax.broadcasted_iota(jnp.int32, (256, 32), 1), 1.0, 0.0
    ).astype(BF)
    p_row = (lax.broadcasted_iota(jnp.int32, (256, 128), 0) % 8).astype(F32)
    p_lane = (lax.broadcasted_iota(jnp.int32, (128, 256), 1) % 8).astype(F32)

    def expand(h, d, ref):
        both = ref[...]
        sel[h, d] = jnp.where(dot(grow, both[:, :128]) == p_row, 1.0, 0.0).astype(BF)
        wide = lax.dot_general(both, grow, (((0,), (1,)), ((), ())), preferred_element_type=F32)
        comb_w[h, d] = jnp.where(wide[:128] == p_lane, wide[128:], 0.0).astype(BF)

    for h in (0, 1):
        expand(h, 0, mw_src.at[h, 0])

    loads[7].wait()
    loads[8].wait()

    def project(d):
        proj[(z - d) % 4] = dot(att[...], wfull[d].reshape(1024, 256))

    project(0)
    f_cp = {}
    for d in NEAR:
        w_cp[d].wait_recv()
        f_cp[d] = remote(wfull.at[d, c], wfull.at[d, c], f_s.at[d - 1], f_r.at[d - 1], at(0, 0, 0, 1))
        if d == 1:
            for dd in NEAR:
                for h in (0, 1):
                    m_cp[h, dd].wait_recv()
                    expand(h, dd, mw_rcv.at[h, dd - 1])
        if d == 3:
            f_cp[1].wait_recv()
            project(1)
    f_cp[3].wait_recv()
    project(3)
    f_cp[2].wait_recv()
    project(2)

    for cp in loads[9:12]:
        cp.wait()
    total = jnp.zeros((128, 1), F32)
    for q in range(4):
        cols = slice(q * 256, q * 256 + 256)
        part = (res[:, cols].astype(F32) + proj[q]).astype(BF)
        hid[:, cols] = part
        wide = part.astype(F32)
        total = total + jnp.sum(wide * wide, axis=1, keepdims=True)
    scale = lax.rsqrt(total * (1.0 / 1024.0) + 1e-06)
    for q in range(4):
        cols = slice(q * 256, q * 256 + 256)
        src1[q // 2, :, (q % 2) * 256 : (q % 2) * 256 + 256] = (
            hid[:, cols].astype(F32) * scale * pre[:, cols]
        ).astype(BF)

    a_cp = {}
    for d in FAR:
        for h in (0, 1):
            a_cp[h, d] = remote(src1.at[h], s1.at[h, d - 1], a_s.at[h, d - 1], a_r.at[h, d - 1], along(h, d, 0))

    def compact(h, d, rows):
        comp[h, :, d] = dot(sel[h, d], rows[...]).astype(BF).reshape(8, 32, 512)

    for h in (0, 1):
        compact(h, 0, src1.at[h])
    for d in NEAR:
        for h in (0, 1):
            a_cp[h, d].wait_recv()
            compact(h, d, s1.at[h, d - 1])

    d_cp = {}
    for dc in (0, 1):
        for d in FAR if dc == 0 else FAR + (0,):
            for h in (0, 1):
                i = dc * 4 + d
                d_cp[h, i] = remote(
                    comp.at[h, i], rec.at[h, i], d_s.at[h, i - 1], d_r.at[h, i - 1], along(1 - h, d, dc)
                )

    loads[12].wait()
    loads[13].wait()
    e_cp = {}
    for dc in (0, 1):
        for d in range(4):
            for h in (0, 1):
                if dc * 4 + d:
                    d_cp[h, dc * 4 + d].wait_recv()

        def got(h, i):
            return comp[h, 0] if i == 0 else rec[h, i]

        for pair in (0, 1):
            xa, xb = [], []
            for dy in (2 * pair, 2 * pair + 1):
                xa.append(got(0, dc * 4 + dy).reshape(128, 512))
                for dx in range(4):
                    xb.append(comp[1, 0, dy] if dc * 4 + dx == 0 else rec[1, dc * 4 + dx, dy])
            xa = jnp.concatenate(xa, axis=0)
            xb = jnp.concatenate(xb, axis=0)
            gate = dot(xa, gu[:512, :512]) + dot(xb, gu[512:, :512])
            up = dot(xa, gu[:512, 512:]) + dot(xb, gu[512:, 512:])
            inner = (gate / (1.0 + jnp.exp(-gate)) * up).astype(BF)
            made = dot(inner, dn[...]).astype(BF)
            for k in (0, 1):
                dy = 2 * pair + k
                ob[0, dc * 4 + dy] = made[k * 128 : k * 128 + 128, :512].reshape(4, 32, 512)
                for dx in range(4):
                    ob[1, dc * 4 + dx, dy] = made[k * 128 + dx * 32 : k * 128 + dx * 32 + 32, 512:]
        for d in FAR if dc == 0 else FAR + (0,):
            for h in (0, 1):
                i = dc * 4 + d
                e_cp[h, i] = remote(
                    ob.at[h, i], comb.at[h, i], e_s.at[h, i - 1], e_r.at[h, i - 1], along(1 - h, 4 - d, dc)
                )

    for dc in (0, 1):
        for d in range(4):
            for h in (0, 1):
                if dc * 4 + d:
                    e_cp[h, dc * 4 + d].wait_recv()

    def summed(h, d):
        back = jnp.concatenate([ob[h, 0, d]] + [comb[h, i, d] for i in range(1, 8)], axis=0)
        return dot(comb_w[h, d], back)

    p_cp = {}
    for d in FAR:
        for h in (0, 1):
            part_src[h, d - 1] = summed(h, d).astype(BF)
            p_cp[h, d] = remote(
                part_src.at[h, d - 1], part_rcv.at[h, d - 1], p_s.at[h, d - 1], p_r.at[h, d - 1], along(h, 4 - d, 0)
            )
    values = []
    total = jnp.zeros((128, 1), F32)
    for h in (0, 1):
        mix = summed(h, 0)
        for d in NEAR:
            p_cp[h, d].wait_recv()
            mix = mix + part_rcv[h, d - 1].astype(F32)
        v = hid[:, h * 512 : h * 512 + 512].astype(F32) + mix
        total = total + jnp.sum(v * v, axis=1, keepdims=True)
        values.append(v)
    scale = lax.rsqrt(total * (1.0 / 1024.0) + 1e-06)
    for h in (0, 1):
        cols = slice(h * 512, h * 512 + 512)
        out_ref[:, cols] = (values[h] * scale * post[:, cols]).astype(BF)
    for cp in sends:
        cp.wait_send()


def on_device(
    attention, residual, out_proj, pre_gain, post_gain, slot_gate_up, slot_down, expert_ids, copy_choice,
    placement, request_age, decode_flag, capacity, route_weight,
):
    dma = pltpu.SemaphoreType.DMA
    vm = pltpu.VMEM
    return pl.pallas_call(
        kernel,
        out_shape=jax.ShapeDtypeStruct((128, 1024), BF),
        in_specs=[pl.BlockSpec(memory_space=pl.ANY)] * 14,
        out_specs=pl.BlockSpec(memory_space=pltpu.VMEM),
        scratch_shapes=[
            vm((128, 1024), BF), vm((128, 1024), BF), vm((1, 1024), F32), vm((1, 1024), F32),
            vm((1024, 1024), BF), vm((512, 1024), BF),
            vm((8, 128), jnp.int32), vm((8, 128), jnp.int32), vm((1, 32), jnp.int32),
            vm((1, 128), jnp.int32), vm((1, 128), jnp.int32), vm((4, 32), jnp.int32), vm((8, 128), F32),
            vm((4, 2, 512, 256), BF), vm((4, 128, 256), F32), vm((128, 1024), BF),
            vm((2, 128, 512), BF), vm((2, 3, 128, 512), BF),
            vm((2, 4, 32, 256), BF), vm((2, 3, 32, 256), BF),
            vm((2, 4, 256, 128), BF), vm((2, 4, 128, 256), BF),
            vm((2, 8, 4, 32, 512), BF), vm((2, 8, 4, 32, 512), BF),
            vm((2, 8, 4, 32, 512), BF), vm((2, 8, 4, 32, 512), BF),
            vm((2, 3, 128, 512), BF), vm((2, 3, 128, 512), BF),
            dma((14,)),
            dma((3,)), dma((3,)), dma((3,)), dma((3,)),
            dma((2, 3)), dma((2, 3)), dma((2, 3)), dma((2, 3)),
            dma((2, 7)), dma((2, 7)), dma((2, 7)), dma((2, 7)),
            dma((2, 3)), dma((2, 3)),
        ],
        compiler_params=pltpu.CompilerParams(
            collective_id=0, has_side_effects=True, vmem_limit_bytes=67_000_000
        ),
        cost_estimate=pl.CostEstimate(flops=4_000_000_000, bytes_accessed=5_000_000, transcendentals=600_000),
        name="moe_layer",
    )(
        attention, residual, out_proj.reshape(2, 512, 256), pre_gain.reshape(1, -1), post_gain.reshape(1, -1),
        slot_gate_up[0], slot_down[0], expert_ids.T, copy_choice.T, placement.reshape(1, -1),
        request_age.reshape(1, -1), decode_flag.reshape(1, -1), capacity, route_weight.T,
    )


def solution(mesh):
    rows = P(("grp", "ep"), None)
    placed = (
        rows, rows, P(None, "grp"), P(), P(), P("ep", None, None), P("ep", None, None), rows, rows, P(),
        P(("grp", "ep")), P(("grp", "ep")), P(), rows,
    )
    return jax.shard_map(on_device, mesh=mesh, in_specs=placed, out_specs=rows, check_vma=False)
```

```python
import jax
import jax.numpy as jnp
from jax import lax
from jax.experimental import pallas as pl
from jax.experimental.pallas import tpu as pltpu
from jax.sharding import PartitionSpec as P

MESH = pl.DeviceIdType.MESH
BF = jnp.bfloat16
F32 = jnp.float32
DIST = (0, 1, 3, 2)


def dot(a, b):
    return jnp.dot(a, b, preferred_element_type=F32)


def kernel(
    att_h, res_h, wo_h, pre_h, post_h, gu_h, dn_h, ids_h, cc_h, place_h, age_h, flag_h, cap_h, rw_h,
    out_ref,
    pre, post, gu, dn, ids, cc, place, age, flag, cap, rw,
    att, res, wmine, hall, hfin, mw_src, mw_all, sel, comb_w, ss_src, ss_rcv,
    comp, comp2, rec, rec2, ob, comb, part_src, part_rcv,
    in_sem, loc_sem, w_s, w_r, a_s, a_r, r_s, r_r, m_s, m_r, h_s, h_r, q_s, q_r, d_s, d_r, e_s, e_r, p_s, p_r,
):
    z = lax.axis_index("grp")
    e = lax.axis_index("ep")
    x, y, c = e // 8, (e // 2) % 4, e % 2
    other = 1 - c

    def dev(dx, dy, core):
        return (z, (((x + dx) % 4) * 4 + (y + dy) % 4) * 2 + core)

    def first(d, core):
        return dev(d * other, d * c, core)

    def second(d, core):
        return dev(d * c, d * other, core)

    bar = pltpu.get_barrier_semaphore()
    greet = [((z + d) % 4, e) for d in (1, 2, 3)] + [dev(0, 0, other)]
    for d in (1, 2, 3):
        for core in (0, 1):
            greet += [dev(d, 0, core), dev(0, d, core)]
    for to in greet:
        pl.semaphore_signal(bar, inc=1, device_id=to, device_id_type=MESH)

    def half_of(half):
        return pl.ds(pl.multiple_of(half * 512, 512), 512)

    loads = []
    for i, (src, dst) in enumerate(
        (
            (ids_h, ids), (cc_h, cc), (place_h, place), (age_h, age), (flag_h, flag), (cap_h, cap), (rw_h, rw),
            (att_h, att.at[0, c]), (res_h.at[:, half_of(c)], res.at[0, c]), (pre_h, pre), (post_h, post),
            (gu_h, gu), (dn_h, dn),
        )
    ):
        cp = pltpu.make_async_copy(src, dst, in_sem.at[i])
        cp.start()
        loads.append(cp)
    has_w = c == z // 2
    w_local = pltpu.make_async_copy(wo_h, wmine.at[z % 2], in_sem.at[13])

    sends = []

    def remote(src, dst, ss, rs, to):
        cp = pltpu.make_async_remote_copy(
            src_ref=src, dst_ref=dst, send_sem=ss, recv_sem=rs, device_id=to, device_id_type=MESH
        )
        cp.start()
        sends.append(cp)

    def arrived(dst, rs):
        pltpu.make_async_remote_copy(
            src_ref=dst, dst_ref=dst, send_sem=rs, recv_sem=rs, device_id=dev(0, 0, other), device_id_type=MESH
        ).wait_recv()

    w_cp = [
        pltpu.make_async_remote_copy(
            src_ref=wo_h, dst_ref=wmine.at[z % 2], send_sem=w_s.at[d - 1], recv_sem=w_r.at[z % 2],
            device_id=((z + d) % 4, e), device_id_type=MESH,
        )
        for d in (2, 1, 3)
    ]
    pl.semaphore_wait(bar, len(greet))

    @pl.when(has_w)
    def _():
        w_local.start()
        for cp in w_cp:
            cp.start()

    k = 0
    for p in (1, 2):
        d = DIST[p]
        for half, to in ((0, dev(d, 0, 0)), (1, dev(0, d, 1))):
            remote(att_h, att.at[p, c], a_s.at[k], a_r.at[p, c], to)
            remote(res_h.at[:, half * 512 : half * 512 + 512], res.at[p, c], r_s.at[k], r_r.at[p, c], to)
            k += 1
    remote(att_h, att.at[0, c], a_s.at[k], a_r.at[0, c], dev(0, 0, other))
    remote(res_h.at[:, half_of(other)], res.at[0, c], r_s.at[k], r_r.at[0, c], dev(0, 0, other))

    for cp in loads[:7]:
        cp.wait()
    row = lax.broadcasted_iota(jnp.int32, (128, 128), 0)
    lane = lax.broadcasted_iota(jnp.int32, (128, 128), 1)
    eye = row == lane
    pr_row = (flag[...] * 1048576 + age[...]).astype(F32)
    pr_col = jnp.sum(jnp.where(eye, pr_row, 0.0), axis=1, keepdims=True)
    ahead = jnp.where((pr_col > pr_row) | ((pr_col == pr_row) & (row < lane)), 1.0, 0.0)
    t = lax.broadcasted_iota(jnp.int32, (128, 32), 0)
    slot_lane = lax.broadcasted_iota(jnp.int32, (128, 32), 1)
    copy_of = t % 4
    px, py = t // 32, (t // 4) % 4
    dx = jnp.where(px < 2, px, 5 - px)
    dy = jnp.where(py < 2, py, 5 - py)
    slot = (((x + dx) % 4) * 4 + (y + dy) % 4) * 2 + (t // 16) % 2
    here = slot_lane == slot
    expert = jnp.sum(jnp.where(here, place[...].astype(F32), 0.0), axis=1, keepdims=True)
    code_col = expert * 4.0 + copy_of[:, :1].astype(F32)
    capf = cap[...].astype(F32)
    cap_sel = jnp.zeros((128, 32), F32)
    for g in range(4):
        cap_sel = jnp.where(here & (copy_of == g), capf[g : g + 1, :], cap_sel)
    cap_col = jnp.sum(cap_sel, axis=1, keepdims=True)
    code = (ids[...] * 4 + cc[...]).astype(F32)
    hits = jnp.zeros((128, 128), F32)
    weight = jnp.zeros((128, 128), F32)
    for i in range(8):
        same = code_col == code[i : i + 1, :]
        hits = jnp.where(same, 1.0, hits)
        weight = jnp.where(same, rw[i : i + 1, :], weight)
    counts = dot(hits.astype(BF), ahead.astype(BF))
    place_in = jnp.where((hits > 0.5) & (counts < cap_col), counts, 99.0)
    pw = jnp.concatenate([place_in, weight], axis=1)
    for p in range(4):
        mw_src[0, p] = pw[p * 32 : p * 32 + 32].astype(BF)
        blocks = []
        for core in range(2):
            for q in range(4):
                lo = q * 32 + core * 16 + p * 4
                blocks.append(pw[lo : lo + 4])
        mw_src[1, p] = jnp.concatenate(blocks, axis=0).astype(BF)
    k = 0
    for p in (1, 2, 3):
        d = DIST[p]
        for half, to in ((0, dev(d, 0, 0)), (1, dev(0, d, 1))):
            remote(mw_src.at[half, p], mw_all.at[p, c], m_s.at[k], m_r.at[p, c], to)
            k += 1
    remote(mw_src.at[other, 0], mw_all.at[0, c], m_s.at[k], m_r.at[0, c], dev(0, 0, other))
    mw_all[0, c] = mw_src[c, 0]

    grow = jnp.where(
        lax.broadcasted_iota(jnp.int32, (256, 32), 0) // 8 == lax.broadcasted_iota(jnp.int32, (256, 32), 1), 1.0, 0.0
    ).astype(BF)
    p_row = (lax.broadcasted_iota(jnp.int32, (256, 128), 0) % 8).astype(F32)
    p_lane = (lax.broadcasted_iota(jnp.int32, (128, 256), 1) % 8).astype(F32)
    arrived(mw_all.at[0, other], m_r.at[0, other])
    for p in range(4):
        for core in (0, 1):
            if p:
                arrived(mw_all.at[p, core], m_r.at[p, core])
            both = mw_all[p, core]
            sel[p, core] = jnp.where(dot(grow, both[:, :128]) == p_row, 1.0, 0.0).astype(BF)
            wide = lax.dot_general(both, grow, (((0,), (1,)), ((), ())), preferred_element_type=F32)
            comb_w[p, core] = jnp.where(wide[:128] == p_lane, wide[128:], 0.0).astype(BF)

    for cp in loads[7:]:
        cp.wait()
    arrived(att.at[0, other], a_r.at[0, other])
    arrived(res.at[0, other], r_r.at[0, other])

    @pl.when(has_w)
    def _():
        w_local.wait()

    for q in (0, 1):

        @pl.when(c * 2 + q != z)
        def _():
            arrived(wmine.at[q], w_r.at[q])

    def project(p):
        rows = att[p].reshape(256, 1024)
        for q in (0, 1):
            cols = slice(q * 256, q * 256 + 256)
            part = dot(rows, wmine[q]).reshape(2, 128, 256)
            hall[p, :, :, cols] = (res[p, :, :, cols].astype(F32) + part).astype(BF)

    def squares(p, core):
        wide = hall[p, core].astype(F32)
        return jnp.sum(wide * wide, axis=1, keepdims=True)

    project(0)
    remote(hall.at[0], hall.at[3], h_s.at[0], h_r.at[0], first(2, c))
    remote(hall.at[0, other], hfin.at[c], h_s.at[1], h_r.at[1], dev(0, 0, other))
    own_ss = {}
    for core in (0, 1):
        own_ss[0, core] = squares(0, core)
        ss_src[core : core + 1, :] = jnp.sum(jnp.where(eye, own_ss[0, core], 0.0), axis=0, keepdims=True)
    remote(ss_src, ss_rcv.at[0], q_s.at[0], q_r.at[0], dev(0, 0, other))
    for p in (1, 2, 3):
        remote(ss_src, ss_rcv.at[p], q_s.at[p], q_r.at[p], second(DIST[p], other))
    hfin[c] = hall[0, c]
    for p in (1, 2):
        for core in (0, 1):
            arrived(att.at[p, core], a_r.at[p, core])
            arrived(res.at[p, core], r_r.at[p, core])
        project(p)
        for core in (0, 1):
            own_ss[p, core] = squares(p, core)

    gain = pre[c]

    def compact(p, core):
        total = own_ss[p, core] + jnp.sum(jnp.where(eye, ss_rcv[p, core : core + 1, :], 0.0), axis=1, keepdims=True)
        scale = lax.rsqrt(total * (1.0 / 1024.0) + 1e-06)
        normed = (hall[p, core].astype(F32) * scale * gain).astype(BF)
        return dot(sel[p, core], normed).astype(BF).reshape(2, 4, 32, 512)

    local = []

    def spread(src, dst, kind):
        for p in (3, 1, 2):
            for core in (0, 1):
                remote(
                    src.at[core, p], dst(p), d_s.at[kind, core * 3 + p - 1], d_r.at[kind, c * 3 + p - 1],
                    second(DIST[p], core),
                )
        remote(src.at[other, 0], dst(0), d_s.at[kind, 6], d_r.at[kind, 6], dev(0, 0, other))
        cp = pltpu.make_async_copy(src.at[c, 0], dst(0), loc_sem.at[kind])
        cp.start()
        local.append(cp)

    for p in range(3):
        arrived(ss_rcv.at[p], q_r.at[p])
        comp[0, :, :, p] = compact(p, 0)
    spread(comp.at[0], lambda p: rec.at[c, p, 0], 0)
    arrived(hall.at[3], h_r.at[0])
    arrived(ss_rcv.at[3], q_r.at[3])
    for core in (0, 1):
        own_ss[3, core] = squares(3, core)
        comp2[:, :, core] = compact(3, core)
    spread(comp2, lambda p: rec2.at[c, p], 1)
    for p in range(3):
        comp[1, :, :, p] = compact(p, 1)
    spread(comp.at[1], lambda p: rec.at[c, p, 1], 2)

    def places_in(src, kind):
        for half in (0, 1):
            for p in (1, 2, 3):
                arrived(src(half, p), d_r.at[kind, half * 3 + p - 1])
        arrived(src(other, 0), d_r.at[kind, 6])
        local[kind].wait()

    back = []
    for rows_of in (0, 1):
        if rows_of == 0:
            places_in(lambda half, p: rec.at[half, p, 0], 0)
            places_in(lambda half, p: rec2.at[half, p], 1)
        else:
            places_in(lambda half, p: rec.at[half, p, 1], 2)

        def got(half, p, q):
            return rec2[half, p, rows_of] if q == 3 else rec[half, p, rows_of, q]

        for pair in (0, 1):
            blocks = [(qy, qx) for qy in (2 * pair, 2 * pair + 1) for qx in range(4)]
            xa = jnp.concatenate([got(0, qy, qx) for qy, qx in blocks], axis=0)
            xb = jnp.concatenate([got(1, qx, qy) for qy, qx in blocks], axis=0)
            gate = dot(xa, gu[:512, :512]) + dot(xb, gu[512:, :512])
            up = dot(xa, gu[:512, 512:]) + dot(xb, gu[512:, 512:])
            inner = (gate / (1.0 + jnp.exp(-gate)) * up).astype(BF)
            made = dot(inner, dn[...]).astype(BF)
            for i, (qy, qx) in enumerate(blocks):
                ob[0, qy, rows_of, qx] = made[i * 32 : i * 32 + 32, :512]
                ob[1, qx, rows_of, qy] = made[i * 32 : i * 32 + 32, 512:]
        for p in (3, 1, 2):
            d = 4 - DIST[p]
            for half, to in ((0, dev(0, d, 0)), (1, dev(d, 0, 1))):
                remote(
                    ob.at[half, p, rows_of], comb.at[p, c, rows_of], e_s.at[rows_of, half * 3 + p - 1],
                    e_r.at[rows_of, c * 3 + p - 1], to,
                )
        remote(
            ob.at[other, 0, rows_of], comb.at[0, c, rows_of], e_s.at[rows_of, 6], e_r.at[rows_of, 6], dev(0, 0, other)
        )
        cp = pltpu.make_async_copy(ob.at[c, 0, rows_of], comb.at[0, c, rows_of], loc_sem.at[3 + rows_of])
        cp.start()
        back.append(cp)

    for rows_of in (0, 1):
        for core in (0, 1):
            for p in (1, 2, 3):
                arrived(comb.at[p, core, rows_of], e_r.at[rows_of, core * 3 + p - 1])
        arrived(comb.at[0, other, rows_of], e_r.at[rows_of, 6])
        back[rows_of].wait()
        for p in (3, 1, 2, 0):
            rows = jnp.concatenate([comb[q, core, rows_of, p] for core in (0, 1) for q in range(4)], axis=0)
            part_src[p, rows_of] = dot(comb_w[p, rows_of], rows).astype(BF)
            if p:
                remote(
                    part_src.at[p, rows_of], part_rcv.at[c, p], p_s.at[rows_of * 3 + p - 1], p_r.at[c * 3 + p - 1],
                    first(4 - DIST[p], rows_of),
                )
    remote(part_src.at[0, other], part_rcv.at[c, 0], p_s.at[6], p_r.at[6], dev(0, 0, other))
    part_rcv[c, 0] = part_src[0, c]
    arrived(hfin.at[other], h_r.at[1])
    arrived(part_rcv.at[other, 0], p_r.at[6])
    values = []
    total = jnp.zeros((128, 1), F32)
    for half in (0, 1):
        v = hfin[half].astype(F32) + part_rcv[half, 0].astype(F32)
        for p in (1, 2, 3):
            arrived(part_rcv.at[half, p], p_r.at[half * 3 + p - 1])
            v = v + part_rcv[half, p].astype(F32)
        total = total + jnp.sum(v * v, axis=1, keepdims=True)
        values.append(v)
    scale = lax.rsqrt(total * (1.0 / 1024.0) + 1e-06)
    for half in (0, 1):
        cols = slice(half * 512, half * 512 + 512)
        out_ref[:, cols] = (values[half] * scale * post[:, cols]).astype(BF)
    for cp in sends:
        cp.wait_send()

    @pl.when(has_w)
    def _():
        for cp in w_cp:
            cp.wait_send()


def on_device(
    attention, residual, out_proj, pre_gain, post_gain, slot_gate_up, slot_down, expert_ids, copy_choice,
    placement, request_age, decode_flag, capacity, route_weight,
):
    dma = pltpu.SemaphoreType.DMA
    vm = pltpu.VMEM
    return pl.pallas_call(
        kernel,
        out_shape=jax.ShapeDtypeStruct((128, 1024), BF),
        in_specs=[pl.BlockSpec(memory_space=pl.ANY)] * 14,
        out_specs=pl.BlockSpec(memory_space=pltpu.VMEM),
        scratch_shapes=[
            vm((2, 1, 512), F32), vm((1, 1024), F32), vm((1024, 1024), BF), vm((512, 1024), BF),
            vm((8, 128), jnp.int32), vm((8, 128), jnp.int32), vm((1, 32), jnp.int32),
            vm((1, 128), jnp.int32), vm((1, 128), jnp.int32), vm((4, 32), jnp.int32), vm((8, 128), F32),
            vm((3, 2, 128, 1024), BF), vm((3, 2, 128, 512), BF), vm((2, 1024, 256), BF),
            vm((4, 2, 128, 512), BF), vm((2, 128, 512), BF),
            vm((2, 4, 32, 256), BF), vm((4, 2, 32, 256), BF),
            vm((4, 2, 256, 128), BF), vm((4, 2, 128, 256), BF),
            vm((8, 128), F32), vm((4, 8, 128), F32),
            vm((2, 2, 4, 3, 32, 512), BF), vm((2, 4, 2, 32, 512), BF),
            vm((2, 4, 2, 3, 32, 512), BF), vm((2, 4, 2, 32, 512), BF),
            vm((2, 4, 2, 4, 32, 512), BF), vm((4, 2, 2, 4, 32, 512), BF),
            vm((4, 2, 128, 512), BF), vm((2, 4, 128, 512), BF),
            dma((14,)), dma((5,)),
            dma((3,)), dma((2,)),
            dma((5,)), dma((3, 2)), dma((5,)), dma((3, 2)),
            dma((7,)), dma((4, 2)),
            dma((2,)), dma((2,)), dma((4,)), dma((4,)),
            dma((3, 7)), dma((3, 7)), dma((2, 7)), dma((2, 7)), dma((7,)), dma((7,)),
        ],
        compiler_params=pltpu.CompilerParams(
            collective_id=0, has_side_effects=True, vmem_limit_bytes=67_000_000
        ),
        cost_estimate=pl.CostEstimate(flops=5_000_000_000, bytes_accessed=5_000_000, transcendentals=600_000),
        name="moe_layer",
    )(
        attention, residual, out_proj, pre_gain.reshape(2, 1, 512), post_gain.reshape(1, -1),
        slot_gate_up[0], slot_down[0], expert_ids.T, copy_choice.T, placement.reshape(1, -1),
        request_age.reshape(1, -1), decode_flag.reshape(1, -1), capacity, route_weight.T,
    )


def solution(mesh):
    rows = P(("grp", "ep"), None)
    placed = (
        rows, rows, P(None, "grp"), P(), P(), P("ep", None, None), P("ep", None, None), rows, rows, P(),
        P(("grp", "ep")), P(("grp", "ep")), P(), rows,
    )
    return jax.shard_map(on_device, mesh=mesh, in_specs=placed, out_specs=rows, check_vma=False)
```

```python
import jax
import jax.numpy as jnp
from jax import lax
from jax.experimental import pallas as pl
from jax.experimental.pallas import tpu as pltpu
from jax.sharding import PartitionSpec as P

MESH = pl.DeviceIdType.MESH
BF = jnp.bfloat16
F32 = jnp.float32
DIST = (0, 1, 3, 2)


def dot(a, b):
    return jnp.dot(a, b, preferred_element_type=F32)


def kernel(
    att_h, res_h, wo_h, pre_h, post_h, gu_h, dn_h, ids_h, cc_h, place_h, age_h, flag_h, cap_h, rw_h,
    out_ref,
    pre, post, gu, dn, ids, cc, place, age, flag, cap, rw,
    att, res, wmine, hall, hfin, mw_src, mw_all, sel, comb_w, ss_src, ss_rcv,
    comp, rec, ob, comb, part_src, part_rcv,
    in_sem, loc_sem, w_s, w_f, w_r, a_s, a_r, r_s, r_r, m_s, m_r, h_s, h_r, q_s, q_r, d_s, d_r, e_s, e_r, p_s, p_r,
):
    z = lax.axis_index("grp")
    e = lax.axis_index("ep")
    x, y, c = e >> 3, (e >> 1) & 3, e & 1
    other = 1 - c

    def dev(dx, dy, core):
        return (z, ((x + dx) & 3) * 8 + ((y + dy) & 3) * 2 + core)

    def first(d, core):
        return dev(d * other, d * c, core)

    def second(d, core):
        return dev(d * c, d * other, core)

    bar = pltpu.get_barrier_semaphore()
    up, down = ((z + 1) & 3, e), ((z + 3) & 3, e)
    greet = [up, down, dev(0, 0, other)]
    for d in (1, 2, 3):
        for core in (0, 1):
            greet += [dev(d, 0, core), dev(0, d, core)]
    for to in greet:
        pl.semaphore_signal(bar, inc=1, device_id=to, device_id_type=MESH)

    def half_of(half):
        return pl.ds(pl.multiple_of(half * 512, 512), 512)

    sends = []

    def remote(src, dst, ss, rs, to):
        cp = pltpu.make_async_remote_copy(
            src_ref=src, dst_ref=dst, send_sem=ss, recv_sem=rs, device_id=to, device_id_type=MESH
        )
        cp.start()
        sends.append(cp)

    def arrived(dst, rs):
        pltpu.make_async_remote_copy(
            src_ref=dst, dst_ref=dst, send_sem=rs, recv_sem=rs, device_id=dev(0, 0, other), device_id_type=MESH
        ).wait_recv()

    has_w = c == z >> 1
    mine = z & 1
    w_cp = []
    for i, (to, h) in enumerate(((up, 0), (down, 1), (up, 1), (down, 0))):
        w_cp.append(
            pltpu.make_async_remote_copy(
                src_ref=wo_h.at[h], dst_ref=wmine.at[mine, h], send_sem=w_s.at[i], recv_sem=w_r.at[mine, h],
                device_id=to, device_id_type=MESH,
            )
        )
    w_local = pltpu.make_async_copy(wo_h, wmine.at[mine], in_sem.at[13])
    turn = (z - 2 * c) & 3
    near = ((turn + 1) >> 1) & 1
    relays = []
    for t, q, h, to in ((0, 1, 1, down), (1, 0, 0, up), (2, 1, 0, up), (3, 0, 1, down)):
        relays.append(
            (
                t,
                pltpu.make_async_remote_copy(
                    src_ref=wmine.at[q, h], dst_ref=wmine.at[q, h], send_sem=w_f.at[0], recv_sem=w_r.at[q, h],
                    device_id=to, device_id_type=MESH,
                ),
            )
        )
    pl.semaphore_wait(bar, len(greet))

    @pl.when(has_w)
    def _():
        for cp in w_cp:
            cp.start()
        w_local.start()

    k = 0
    for p in (1, 2):
        d = DIST[p]
        for half, to in ((0, dev(d, 0, 0)), (1, dev(0, d, 1))):
            remote(att_h, att.at[p, c], a_s.at[k], a_r.at[p, c], to)
            remote(res_h.at[:, half * 512 : half * 512 + 512], res.at[p, c], r_s.at[k], r_r.at[p, c], to)
            k += 1
    remote(att_h, att.at[0, c], a_s.at[k], a_r.at[0, c], dev(0, 0, other))
    remote(res_h.at[:, half_of(other)], res.at[0, c], r_s.at[k], r_r.at[0, c], dev(0, 0, other))

    loads = []
    for i, (src, dst) in enumerate(
        (
            (ids_h, ids), (cc_h, cc), (place_h, place), (age_h, age), (flag_h, flag), (cap_h, cap), (rw_h, rw),
            (att_h, att.at[0, c]), (res_h.at[:, half_of(c)], res.at[0, c]), (pre_h, pre), (post_h, post),
            (gu_h, gu), (dn_h, dn),
        )
    ):
        cp = pltpu.make_async_copy(src, dst, in_sem.at[i])
        cp.start()
        loads.append(cp)

    for cp in loads[:7]:
        cp.wait()
    row = lax.broadcasted_iota(jnp.int32, (128, 128), 0)
    lane = lax.broadcasted_iota(jnp.int32, (128, 128), 1)
    eye = row == lane
    pr_row = (flag[...] * 1048576 + age[...]).astype(F32)
    pr_col = jnp.sum(jnp.where(eye, pr_row, 0.0), axis=1, keepdims=True)
    ahead = jnp.where((pr_col > pr_row) | ((pr_col == pr_row) & (row < lane)), 1.0, 0.0)
    t = lax.broadcasted_iota(jnp.int32, (128, 32), 0)
    slot_lane = lax.broadcasted_iota(jnp.int32, (128, 32), 1)
    copy_of = t % 4
    px, py = t // 32, (t // 4) % 4
    dx = jnp.where(px < 2, px, 5 - px)
    dy = jnp.where(py < 2, py, 5 - py)
    slot = (((x + dx) % 4) * 4 + (y + dy) % 4) * 2 + (t // 16) % 2
    here = slot_lane == slot
    expert = jnp.sum(jnp.where(here, place[...].astype(F32), 0.0), axis=1, keepdims=True)
    code_col = expert * 4.0 + copy_of[:, :1].astype(F32)
    capf = cap[...].astype(F32)
    cap_sel = jnp.zeros((128, 32), F32)
    for g in range(4):
        cap_sel = jnp.where(here & (copy_of == g), capf[g : g + 1, :], cap_sel)
    cap_col = jnp.sum(cap_sel, axis=1, keepdims=True)
    code = (ids[...] * 4 + cc[...]).astype(F32)
    hits = jnp.zeros((128, 128), F32)
    weight = jnp.zeros((128, 128), F32)
    for i in range(8):
        same = code_col == code[i : i + 1, :]
        hits = jnp.where(same, 1.0, hits)
        weight = jnp.where(same, rw[i : i + 1, :], weight)
    counts = dot(hits.astype(BF), ahead.astype(BF))
    place_in = jnp.where((hits > 0.5) & (counts < cap_col), counts, 99.0)
    pw = jnp.concatenate([place_in, weight], axis=1)
    for p in range(4):
        mw_src[0, p] = pw[p * 32 : p * 32 + 32].astype(BF)
        blocks = []
        for core in range(2):
            for q in range(4):
                lo = q * 32 + core * 16 + p * 4
                blocks.append(pw[lo : lo + 4])
        mw_src[1, p] = jnp.concatenate(blocks, axis=0).astype(BF)
    k = 0
    for p in (1, 2, 3):
        d = DIST[p]
        for half, to in ((0, dev(d, 0, 0)), (1, dev(0, d, 1))):
            remote(mw_src.at[half, p], mw_all.at[p, c], m_s.at[k], m_r.at[p, c], to)
            k += 1
    remote(mw_src.at[other, 0], mw_all.at[0, c], m_s.at[k], m_r.at[0, c], dev(0, 0, other))
    mw_all[0, c] = mw_src[c, 0]

    for t, cp in relays:

        @pl.when(turn == t)
        def _():
            cp.wait_recv()
            cp.start()

    grow = jnp.where(
        lax.broadcasted_iota(jnp.int32, (256, 32), 0) // 8 == lax.broadcasted_iota(jnp.int32, (256, 32), 1), 1.0, 0.0
    ).astype(BF)
    p_row = (lax.broadcasted_iota(jnp.int32, (256, 128), 0) % 8).astype(F32)
    p_lane = (lax.broadcasted_iota(jnp.int32, (128, 256), 1) % 8).astype(F32)
    arrived(mw_all.at[0, other], m_r.at[0, other])
    for p in range(4):
        for core in (0, 1):
            if p:
                arrived(mw_all.at[p, core], m_r.at[p, core])
            both = mw_all[p, core]
            sel[p, core] = jnp.where(dot(grow, both[:, :128]) == p_row, 1.0, 0.0).astype(BF)
            wide = lax.dot_general(both, grow, (((0,), (1,)), ((), ())), preferred_element_type=F32)
            comb_w[p, core] = jnp.where(wide[:128] == p_lane, wide[128:], 0.0).astype(BF)

    def quarter_in(q):
        @pl.when(has_w & (mine == q))
        def _():
            w_local.wait()

        for h in (0, 1):
            relayed = ((0, 1, 1), (1, 0, 0), (2, 1, 0), (3, 0, 1))
            done = [t for t, rq, rh in relayed if rq == q and rh == h]
            waits = ~(has_w & (mine == q))
            for t in done:
                waits = waits & (turn != t)

            @pl.when(waits)
            def _():
                arrived(wmine.at[q, h], w_r.at[q, h])

    def project(p, q):
        rows = att[p].reshape(256, 1024)
        part = dot(rows, wmine[q].reshape(1024, 256)).reshape(2, 128, 256)
        cols = pl.ds(pl.multiple_of(q * 256, 256), 256)
        hall[p, :, :, cols] = (res[p, :, :, cols].astype(F32) + part).astype(BF)

    def squares(p, core):
        wide = hall[p, core].astype(F32)
        return jnp.sum(wide * wide, axis=1, keepdims=True)

    for cp in loads[7:]:
        cp.wait()
    arrived(att.at[0, other], a_r.at[0, other])
    arrived(res.at[0, other], r_r.at[0, other])
    for p in (1, 2):
        for core in (0, 1):
            arrived(att.at[p, core], a_r.at[p, core])
            arrived(res.at[p, core], r_r.at[p, core])
    for q in (0, 1):

        @pl.when(near == q)
        def _():
            quarter_in(q)

    for p in range(3):
        project(p, near)
    for q in (0, 1):

        @pl.when(near != q)
        def _():
            quarter_in(q)

    project(0, 1 - near)
    own_ss = {}
    for core in (0, 1):
        own_ss[0, core] = squares(0, core)
        ss_src[core : core + 1, :] = jnp.sum(jnp.where(eye, own_ss[0, core], 0.0), axis=0, keepdims=True)
    for p in (1, 2, 3):
        remote(ss_src, ss_rcv.at[p], q_s.at[p], q_r.at[p], second(DIST[p], other))
    remote(ss_src, ss_rcv.at[0], q_s.at[0], q_r.at[0], dev(0, 0, other))
    project(1, 1 - near)
    remote(hall.at[1, 0], hall.at[3, 0], h_s.at[0], h_r.at[0], first(1, c))
    project(2, 1 - near)
    remote(hall.at[2, 1], hall.at[3, 1], h_s.at[1], h_r.at[1], first(3, c))
    for p in (1, 2):
        for core in (0, 1):
            own_ss[p, core] = squares(p, core)
    gain = pre[c]

    def compact(p, core):
        own = own_ss[p, core]
        total = own + jnp.sum(jnp.where(eye, ss_rcv[p, core : core + 1, :], 0.0), axis=1, keepdims=True)
        scale = lax.rsqrt(total * (1.0 / 1024.0) + 1e-06)
        normed = (hall[p, core].astype(F32) * scale * gain).astype(BF)
        return dot(sel[p, core], normed).astype(BF).reshape(2, 4, 32, 512)

    local = []

    def part_of(kind):
        return ((0, pl.ds(0, 3)), (0, 3), (1,))[kind]

    def spread(kind):
        for p in (3, 1, 2):
            for core in (0, 1):
                remote(
                    comp.at[(core, p) + part_of(kind)], rec.at[(c, p) + part_of(kind)],
                    d_s.at[kind, core * 3 + p - 1], d_r.at[kind, c * 3 + p - 1], second(DIST[p], core),
                )
        remote(
            comp.at[(other, 0) + part_of(kind)], rec.at[(c, 0) + part_of(kind)], d_s.at[kind, 6], d_r.at[kind, 6],
            dev(0, 0, other),
        )
        cp = pltpu.make_async_copy(
            comp.at[(c, 0) + part_of(kind)], rec.at[(c, 0) + part_of(kind)], loc_sem.at[kind]
        )
        cp.start()
        local.append(cp)

    for p in range(3):
        arrived(ss_rcv.at[p], q_r.at[p])
        comp[:, :, 0, p] = compact(p, 0)
    spread(0)
    arrived(ss_rcv.at[3], q_r.at[3])
    for core in (0, 1):
        arrived(hall.at[3, core], h_r.at[core])
        own_ss[3, core] = squares(3, core)
    comp[:, :, 0, 3] = compact(3, 0)

    spread(1)
    for p in range(4):
        comp[:, :, 1, p] = compact(p, 1)
    spread(2)
    remote(hall.at[0, other], hfin.at[c], h_s.at[2], h_r.at[2], dev(0, 0, other))
    hfin[c] = hall[0, c]

    def places_in(kind):
        for half in (0, 1):
            for p in (1, 2, 3):
                arrived(rec.at[(half, p) + part_of(kind)], d_r.at[kind, half * 3 + p - 1])
        arrived(rec.at[(other, 0) + part_of(kind)], d_r.at[kind, 6])
        local[kind].wait()

    def back_part(kind):
        return ((0,), (1, pl.ds(1, 3)), (1, 0))[kind]

    back = []

    def give_back(kind, half, p):
        d = 4 - DIST[p]
        remote(
            ob.at[(half, p) + back_part(kind)], comb.at[(p, c) + back_part(kind)], e_s.at[kind, half * 3 + p - 1],
            e_r.at[kind, c * 3 + p - 1], dev(0, d, 0) if half == 0 else dev(d, 0, 1),
        )

    def give_chip(kind):
        remote(
            ob.at[(other, 0) + back_part(kind)], comb.at[(0, c) + back_part(kind)], e_s.at[kind, 6], e_r.at[kind, 6],
            dev(0, 0, other),
        )
        cp = pltpu.make_async_copy(
            ob.at[(c, 0) + back_part(kind)], comb.at[(0, c) + back_part(kind)], loc_sem.at[3 + kind]
        )
        cp.start()
        back.append(cp)

    for rows_of in (0, 1):
        if rows_of == 0:
            places_in(0)
            places_in(1)
        else:
            places_in(2)

        for pair in (0, 1):
            blocks = [(qy, qx) for qy in (2 * pair, 2 * pair + 1) for qx in range(4)]
            xa = jnp.concatenate([rec[0, qy, rows_of, qx] for qy, qx in blocks], axis=0)
            xb = jnp.concatenate([rec[1, qx, rows_of, qy] for qy, qx in blocks], axis=0)
            gate = dot(xa, gu[:512, :512]) + dot(xb, gu[512:, :512])
            raised = dot(xa, gu[:512, 512:]) + dot(xb, gu[512:, 512:])
            inner = (gate / (1.0 + jnp.exp(-gate)) * raised).astype(BF)
            made = dot(inner, dn[...]).astype(BF)
            for i, (qy, qx) in enumerate(blocks):
                ob[0, qy, rows_of, qx] = made[i * 32 : i * 32 + 32, :512]
                ob[1, qx, rows_of, qy] = made[i * 32 : i * 32 + 32, 512:]
            if pair == 0:
                give_back(rows_of, 0, 1)
            else:
                for half, p in ((0, 3), (1, 3), (1, 1), (0, 2), (1, 2)):
                    give_back(rows_of, half, p)
        give_chip(rows_of)
    for p in (3, 1, 2):
        for half in (0, 1):
            give_back(2, half, p)
    give_chip(2)

    def results_in(kind):
        for core in (0, 1):
            for p in (1, 2, 3):
                arrived(comb.at[(p, core) + back_part(kind)], e_r.at[kind, core * 3 + p - 1])
        arrived(comb.at[(0, other) + back_part(kind)], e_r.at[kind, 6])
        back[kind].wait()

    def weigh(p, rows_of):
        rows = jnp.concatenate([comb[q, core, rows_of, p] for core in (0, 1) for q in range(4)], axis=0)
        part_src[p, rows_of] = dot(comb_w[p, rows_of], rows).astype(BF)

    for rows_of in (0, 1):
        results_in(rows_of)
        for p in (3, 1, 2):
            weigh(p, rows_of)
            remote(
                part_src.at[p, rows_of], part_rcv.at[c, p], p_s.at[rows_of * 3 + p - 1], p_r.at[c * 3 + p - 1],
                first(4 - DIST[p], rows_of),
            )
    weigh(0, 0)
    results_in(2)
    weigh(0, 1)
    remote(part_src.at[0, other], part_rcv.at[c, 0], p_s.at[6], p_r.at[6], dev(0, 0, other))
    part_rcv[c, 0] = part_src[0, c]
    arrived(hfin.at[other], h_r.at[2])
    arrived(part_rcv.at[other, 0], p_r.at[6])
    values = []
    total = jnp.zeros((128, 1), F32)
    for half in (0, 1):
        v = hfin[half].astype(F32) + part_rcv[half, 0].astype(F32)
        for p in (1, 2, 3):
            arrived(part_rcv.at[half, p], p_r.at[half * 3 + p - 1])
            v = v + part_rcv[half, p].astype(F32)
        total = total + jnp.sum(v * v, axis=1, keepdims=True)
        values.append(v)
    scale = lax.rsqrt(total * (1.0 / 1024.0) + 1e-06)
    for half in (0, 1):
        cols = slice(half * 512, half * 512 + 512)
        out_ref[:, cols] = (values[half] * scale * post[:, cols]).astype(BF)
    for cp in sends:
        cp.wait_send()

    @pl.when(has_w)
    def _():
        for cp in w_cp:
            cp.wait_send()

    relays[0][1].wait_send()


def on_device(
    attention, residual, out_proj, pre_gain, post_gain, slot_gate_up, slot_down, expert_ids, copy_choice,
    placement, request_age, decode_flag, capacity, route_weight,
):
    dma = pltpu.SemaphoreType.DMA
    vm = pltpu.VMEM
    done = pl.pallas_call(
        kernel,
        out_shape=jax.ShapeDtypeStruct((128, 1024), BF),
        in_specs=[pl.BlockSpec(memory_space=pl.ANY)] * 14,
        out_specs=pl.BlockSpec(memory_space=pltpu.VMEM),
        scratch_shapes=[
            vm((2, 1, 512), F32), vm((1, 1024), F32), vm((1024, 1024), BF), vm((512, 1024), BF),
            vm((8, 128), jnp.int32), vm((8, 128), jnp.int32), vm((1, 32), jnp.int32),
            vm((1, 128), jnp.int32), vm((1, 128), jnp.int32), vm((4, 32), jnp.int32), vm((8, 128), F32),
            vm((3, 2, 128, 1024), BF), vm((3, 2, 128, 512), BF), vm((2, 2, 512, 256), BF),
            vm((4, 2, 128, 512), BF), vm((2, 128, 512), BF),
            vm((2, 4, 32, 256), BF), vm((4, 2, 32, 256), BF),
            vm((4, 2, 256, 128), BF), vm((4, 2, 128, 256), BF),
            vm((8, 128), F32), vm((4, 8, 128), F32),
            vm((2, 4, 2, 4, 32, 512), BF), vm((2, 4, 2, 4, 32, 512), BF),
            vm((2, 4, 2, 4, 32, 512), BF), vm((4, 2, 2, 4, 32, 512), BF),
            vm((4, 2, 128, 512), BF), vm((2, 4, 128, 512), BF),
            dma((14,)), dma((6,)),
            dma((4,)), dma((1,)), dma((2, 2)),
            dma((5,)), dma((3, 2)), dma((5,)), dma((3, 2)),
            dma((7,)), dma((4, 2)),
            dma((3,)), dma((3,)), dma((4,)), dma((4,)),
            dma((3, 7)), dma((3, 7)), dma((3, 7)), dma((3, 7)), dma((7,)), dma((7,)),
        ],
        compiler_params=pltpu.CompilerParams(
            collective_id=0, has_side_effects=True, vmem_limit_bytes=67_000_000
        ),
        cost_estimate=pl.CostEstimate(flops=5_000_000_000, bytes_accessed=5_000_000, transcendentals=600_000),
        name="moe_layer",
    )(
        attention, residual, out_proj.reshape(2, 512, 256), pre_gain.reshape(2, 1, 512), post_gain.reshape(1, -1),
        slot_gate_up[0], slot_down[0], expert_ids.T, copy_choice.T, placement.reshape(1, -1),
        request_age.reshape(1, -1), decode_flag.reshape(1, -1), capacity, route_weight.T,
    )
    return done


def solution(mesh):
    rows = P(("grp", "ep"), None)
    placed = (
        rows, rows, P(None, "grp"), P(), P(), P("ep", None, None), P("ep", None, None), rows, rows, P(),
        P(("grp", "ep")), P(("grp", "ep")), P(), rows,
    )
    return jax.shard_map(on_device, mesh=mesh, in_specs=placed, out_specs=rows, check_vma=False)
```

```python
import jax
import jax.numpy as jnp
from jax import lax
from jax.experimental import pallas as pl
from jax.experimental.pallas import tpu as pltpu
from jax.sharding import PartitionSpec as P

MESH = pl.DeviceIdType.MESH
BF = jnp.bfloat16
F32 = jnp.float32
DIST = (0, 1, 3, 2)
ONE, TWO = 1, 0


def dot(a, b):
    return jnp.dot(a, b, preferred_element_type=F32)


def kernel(
    att_h, res_h, wo_h, pre_h, post_h, gu_h, dn_h, ids_h, cc_h, place_h, age_h, flag_h, cap_h, rw_h,
    out_ref,
    pre, post, gu, dn, ids, cc, place, age, flag, cap, rw,
    att, res, wmine, hall, hfin, mw_src, mw_all, sel, comb_w, ss_src, ss_rcv,
    comp, rec, ob, comb, part_src, part_rcv,
    in_sem, loc_sem, w_s, w_f, w_r, a_s, a_r, r_s, r_r, m_s, m_r, h_s, h_r, q_s, q_r, d_s, d_r, e_s, e_r, p_s, p_r,
):
    z = lax.axis_index("grp")
    e = lax.axis_index("ep")
    x, y, c = e >> 3, (e >> 1) & 3, e & 1
    other = 1 - c

    def dev(dx, dy, core):
        return (z, ((x + dx) & 3) * 8 + ((y + dy) & 3) * 2 + core)

    def first(d, core):
        return dev(d * other, d * c, core)

    def second(d, core):
        return dev(d * c, d * other, core)

    bar = pltpu.get_barrier_semaphore()
    up, down = ((z + 1) & 3, e), ((z + 3) & 3, e)
    greet = [up, down, dev(0, 0, other)]
    for d in (1, 2, 3):
        for core in (0, 1):
            greet += [dev(d, 0, core), dev(0, d, core)]
    for to in greet:
        pl.semaphore_signal(bar, inc=1, device_id=to, device_id_type=MESH)

    def half_of(half):
        return pl.ds(pl.multiple_of(half * 512, 512), 512)

    sends = []

    def remote(src, dst, ss, rs, to):
        cp = pltpu.make_async_remote_copy(
            src_ref=src, dst_ref=dst, send_sem=ss, recv_sem=rs, device_id=to, device_id_type=MESH
        )
        cp.start()
        sends.append(cp)

    def arrived(dst, rs):
        pltpu.make_async_remote_copy(
            src_ref=dst, dst_ref=dst, send_sem=rs, recv_sem=rs, device_id=dev(0, 0, other), device_id_type=MESH
        ).wait_recv()

    has_w = c == z >> 1
    mine = z & 1
    w_cp = []
    for i, (to, h) in enumerate(((up, 0), (down, 1), (up, 1), (down, 0))):
        w_cp.append(
            pltpu.make_async_remote_copy(
                src_ref=wo_h.at[h], dst_ref=wmine.at[mine, h], send_sem=w_s.at[i], recv_sem=w_r.at[mine, h],
                device_id=to, device_id_type=MESH,
            )
        )
    w_local = pltpu.make_async_copy(wo_h, wmine.at[mine], in_sem.at[13])
    turn = (z - 2 * c) & 3
    near = ((turn + 1) >> 1) & 1
    relays = []
    for t, q, h, to in ((0, 1, 1, down), (1, 0, 0, up), (2, 1, 0, up), (3, 0, 1, down)):
        relays.append(
            (
                t,
                pltpu.make_async_remote_copy(
                    src_ref=wmine.at[q, h], dst_ref=wmine.at[q, h], send_sem=w_f.at[0], recv_sem=w_r.at[q, h],
                    device_id=to, device_id_type=MESH,
                ),
            )
        )
    pl.semaphore_wait(bar, len(greet))

    @pl.when(has_w)
    def _():
        for cp in w_cp:
            cp.start()
        w_local.start()

    k = 0
    for p in (1, 2):
        d = DIST[p]
        for half, to in ((0, dev(d, 0, 0)), (1, dev(0, d, 1))):
            remote(att_h, att.at[p, c], a_s.at[k], a_r.at[p, c], to)
            remote(res_h.at[:, half * 512 : half * 512 + 512], res.at[p, c], r_s.at[k], r_r.at[p, c], to)
            k += 1
    remote(att_h, att.at[0, c], a_s.at[k], a_r.at[0, c], dev(0, 0, other))
    remote(res_h.at[:, half_of(other)], res.at[0, c], r_s.at[k], r_r.at[0, c], dev(0, 0, other))

    loads = []
    for i, (src, dst) in enumerate(
        (
            (ids_h, ids), (cc_h, cc), (place_h, place), (age_h, age), (flag_h, flag), (cap_h, cap), (rw_h, rw),
            (att_h, att.at[0, c]), (res_h.at[:, half_of(c)], res.at[0, c]), (pre_h, pre), (post_h, post),
            (gu_h, gu), (dn_h, dn),
        )
    ):
        cp = pltpu.make_async_copy(src, dst, in_sem.at[i])
        cp.start()
        loads.append(cp)

    for cp in loads[:7]:
        cp.wait()
    row = lax.broadcasted_iota(jnp.int32, (128, 128), 0)
    lane = lax.broadcasted_iota(jnp.int32, (128, 128), 1)
    eye = row == lane
    pr_row = (flag[...] * 1048576 + age[...]).astype(F32)
    pr_col = jnp.sum(jnp.where(eye, pr_row, 0.0), axis=1, keepdims=True)
    ahead = jnp.where((pr_col > pr_row) | ((pr_col == pr_row) & (row < lane)), 1.0, 0.0)
    t = lax.broadcasted_iota(jnp.int32, (128, 32), 0)
    slot_lane = lax.broadcasted_iota(jnp.int32, (128, 32), 1)
    copy_of = t % 4
    px, py = t // 32, (t // 4) % 4
    dx = jnp.where(px < 2, px, 5 - px)
    dy = jnp.where(py < 2, py, 5 - py)
    slot = (((x + dx) % 4) * 4 + (y + dy) % 4) * 2 + (t // 16) % 2
    here = slot_lane == slot
    expert = jnp.sum(jnp.where(here, place[...].astype(F32), 0.0), axis=1, keepdims=True)
    code_col = expert * 4.0 + copy_of[:, :1].astype(F32)
    capf = cap[...].astype(F32)
    cap_sel = jnp.zeros((128, 32), F32)
    for g in range(4):
        cap_sel = jnp.where(here & (copy_of == g), capf[g : g + 1, :], cap_sel)
    cap_col = jnp.sum(cap_sel, axis=1, keepdims=True)
    code = (ids[...] * 4 + cc[...]).astype(F32)
    hits = jnp.zeros((128, 128), F32)
    weight = jnp.zeros((128, 128), F32)
    for i in range(8):
        same = code_col == code[i : i + 1, :]
        hits = jnp.where(same, 1.0, hits)
        weight = jnp.where(same, rw[i : i + 1, :], weight)
    counts = dot(hits.astype(BF), ahead.astype(BF))
    place_in = jnp.where((hits > 0.5) & (counts < cap_col), counts, 99.0)
    pw = jnp.concatenate([place_in, weight], axis=1)
    for p in range(4):
        mw_src[0, p] = pw[p * 32 : p * 32 + 32].astype(BF)
        blocks = []
        for core in range(2):
            for q in range(4):
                lo = q * 32 + core * 16 + p * 4
                blocks.append(pw[lo : lo + 4])
        mw_src[1, p] = jnp.concatenate(blocks, axis=0).astype(BF)
    k = 0
    for p in (1, 2, 3):
        d = DIST[p]
        for half, to in ((0, dev(d, 0, 0)), (1, dev(0, d, 1))):
            remote(mw_src.at[half, p], mw_all.at[p, c], m_s.at[k], m_r.at[p, c], to)
            k += 1
    remote(mw_src.at[other, 0], mw_all.at[0, c], m_s.at[k], m_r.at[0, c], dev(0, 0, other))
    mw_all[0, c] = mw_src[c, 0]

    for t, cp in relays:

        @pl.when(turn == t)
        def _():
            cp.wait_recv()
            cp.start()

    grow = jnp.where(
        lax.broadcasted_iota(jnp.int32, (256, 32), 0) // 8 == lax.broadcasted_iota(jnp.int32, (256, 32), 1), 1.0, 0.0
    ).astype(BF)
    p_row = (lax.broadcasted_iota(jnp.int32, (256, 128), 0) % 8).astype(F32)
    p_lane = (lax.broadcasted_iota(jnp.int32, (128, 256), 1) % 8).astype(F32)
    arrived(mw_all.at[0, other], m_r.at[0, other])
    for p in range(4):
        for core in (0, 1):
            if p:
                arrived(mw_all.at[p, core], m_r.at[p, core])
            both = mw_all[p, core]
            sel[p, core] = jnp.where(dot(grow, both[:, :128]) == p_row, 1.0, 0.0).astype(BF)
            wide = lax.dot_general(both, grow, (((0,), (1,)), ((), ())), preferred_element_type=F32)
            comb_w[p, core] = jnp.where(wide[:128] == p_lane, wide[128:], 0.0).astype(BF)

    def quarter_in(q):
        @pl.when(has_w & (mine == q))
        def _():
            w_local.wait()

        for h in (0, 1):
            relayed = ((0, 1, 1), (1, 0, 0), (2, 1, 0), (3, 0, 1))
            done = [t for t, rq, rh in relayed if rq == q and rh == h]
            waits = ~(has_w & (mine == q))
            for t in done:
                waits = waits & (turn != t)

            @pl.when(waits)
            def _():
                arrived(wmine.at[q, h], w_r.at[q, h])

    def project(p, q):
        rows = att[p].reshape(256, 1024)
        part = dot(rows, wmine[q].reshape(1024, 256)).reshape(2, 128, 256)
        cols = pl.ds(pl.multiple_of(q * 256, 256), 256)
        hall[p, :, :, cols] = (res[p, :, :, cols].astype(F32) + part).astype(BF)

    def squares(p, core):
        wide = hall[p, core].astype(F32)
        return jnp.sum(wide * wide, axis=1, keepdims=True)

    for cp in loads[7:]:
        cp.wait()
    arrived(att.at[0, other], a_r.at[0, other])
    arrived(res.at[0, other], r_r.at[0, other])
    for p in (1, 2):
        for core in (0, 1):
            arrived(att.at[p, core], a_r.at[p, core])
            arrived(res.at[p, core], r_r.at[p, core])
    for q in (0, 1):

        @pl.when(near == q)
        def _():
            quarter_in(q)

    for p in range(3):
        project(p, near)
    for q in (0, 1):

        @pl.when(near != q)
        def _():
            quarter_in(q)

    project(0, 1 - near)
    own_ss = {}
    for core in (0, 1):
        own_ss[0, core] = squares(0, core)
        ss_src[core : core + 1, :] = jnp.sum(jnp.where(eye, own_ss[0, core], 0.0), axis=0, keepdims=True)
    for p in (1, 2, 3):
        remote(ss_src, ss_rcv.at[p], q_s.at[p], q_r.at[p], second(DIST[p], other))
    remote(ss_src, ss_rcv.at[0], q_s.at[0], q_r.at[0], dev(0, 0, other))
    project(1, 1 - near)
    remote(hall.at[1, 0], hall.at[3, 0], h_s.at[0], h_r.at[0], first(1, c))
    project(2, 1 - near)
    remote(hall.at[2, 1], hall.at[3, 1], h_s.at[1], h_r.at[1], first(3, c))
    for p in (1, 2):
        for core in (0, 1):
            own_ss[p, core] = squares(p, core)
    gain = pre[c]

    def compact(p, core):
        own = own_ss[p, core]
        total = own + jnp.sum(jnp.where(eye, ss_rcv[p, core : core + 1, :], 0.0), axis=1, keepdims=True)
        scale = lax.rsqrt(total * (1.0 / 1024.0) + 1e-06)
        normed = (hall[p, core].astype(F32) * scale * gain).astype(BF)
        return dot(sel[p, core], normed).astype(BF).reshape(2, 4, 32, 512)

    local = []

    def part_of(kind):
        return ((ONE, pl.ds(0, 3)), (ONE, 3), (TWO,))[kind]

    def spread(kind):
        for p in (3, 1, 2):
            for core in (0, 1):
                remote(
                    comp.at[(core, p) + part_of(kind)], rec.at[(c, p) + part_of(kind)],
                    d_s.at[kind, core * 3 + p - 1], d_r.at[kind, c * 3 + p - 1], second(DIST[p], core),
                )
        remote(
            comp.at[(other, 0) + part_of(kind)], rec.at[(c, 0) + part_of(kind)], d_s.at[kind, 6], d_r.at[kind, 6],
            dev(0, 0, other),
        )
        cp = pltpu.make_async_copy(
            comp.at[(c, 0) + part_of(kind)], rec.at[(c, 0) + part_of(kind)], loc_sem.at[kind]
        )
        cp.start()
        local.append(cp)

    for p in range(3):
        arrived(ss_rcv.at[p], q_r.at[p])
        comp[:, :, ONE, p] = compact(p, ONE)
    spread(0)
    arrived(ss_rcv.at[3], q_r.at[3])
    for core in (0, 1):
        arrived(hall.at[3, core], h_r.at[core])
        own_ss[3, core] = squares(3, core)
    comp[:, :, ONE, 3] = compact(3, ONE)

    spread(1)
    for p in range(4):
        comp[:, :, TWO, p] = compact(p, TWO)
    spread(2)
    remote(hall.at[0, other], hfin.at[c], h_s.at[2], h_r.at[2], dev(0, 0, other))
    hfin[c] = hall[0, c]

    def places_in(kind):
        for half in (0, 1):
            for p in (1, 2, 3):
                arrived(rec.at[(half, p) + part_of(kind)], d_r.at[kind, half * 3 + p - 1])
        arrived(rec.at[(other, 0) + part_of(kind)], d_r.at[kind, 6])
        local[kind].wait()

    def back_part(kind):
        return ((ONE,), (TWO, pl.ds(1, 3)), (TWO, 0))[kind]

    back = []

    def give_back(kind, half, p):
        d = 4 - DIST[p]
        remote(
            ob.at[(half, p) + back_part(kind)], comb.at[(p, c) + back_part(kind)], e_s.at[kind, half * 3 + p - 1],
            e_r.at[kind, c * 3 + p - 1], dev(0, d, 0) if half == 0 else dev(d, 0, 1),
        )

    def give_chip(kind):
        remote(
            ob.at[(other, 0) + back_part(kind)], comb.at[(0, c) + back_part(kind)], e_s.at[kind, 6], e_r.at[kind, 6],
            dev(0, 0, other),
        )
        cp = pltpu.make_async_copy(
            ob.at[(c, 0) + back_part(kind)], comb.at[(0, c) + back_part(kind)], loc_sem.at[3 + kind]
        )
        cp.start()
        back.append(cp)

    for step, rows_of in ((0, ONE), (1, TWO)):
        if step == 0:
            places_in(0)
            places_in(1)
        else:
            places_in(2)

        for pair in (0, 1):
            blocks = [(qy, qx) for qy in (2 * pair, 2 * pair + 1) for qx in range(4)]
            xa = jnp.concatenate([rec[0, qy, rows_of, qx] for qy, qx in blocks], axis=0)
            xb = jnp.concatenate([rec[1, qx, rows_of, qy] for qy, qx in blocks], axis=0)
            gate = dot(xa, gu[:512, :512]) + dot(xb, gu[512:, :512])
            raised = dot(xa, gu[:512, 512:]) + dot(xb, gu[512:, 512:])
            inner = (gate / (1.0 + jnp.exp(-gate)) * raised).astype(BF)
            made = dot(inner, dn[...]).astype(BF)
            for i, (qy, qx) in enumerate(blocks):
                ob[0, qy, rows_of, qx] = made[i * 32 : i * 32 + 32, :512]
                ob[1, qx, rows_of, qy] = made[i * 32 : i * 32 + 32, 512:]
            if pair == 0:
                give_back(step, 0, 1)
            else:
                for half, p in ((0, 3), (1, 3), (1, 1), (0, 2), (1, 2)):
                    give_back(step, half, p)
        give_chip(step)
    for p in (3, 1, 2):
        for half in (0, 1):
            give_back(2, half, p)
    give_chip(2)

    before = len(sends)

    def results_in(kind):
        for core in (0, 1):
            for p in (1, 2, 3):
                arrived(comb.at[(p, core) + back_part(kind)], e_r.at[kind, core * 3 + p - 1])
        arrived(comb.at[(0, other) + back_part(kind)], e_r.at[kind, 6])
        back[kind].wait()

    def weigh(p, rows_of):
        rows = jnp.concatenate([comb[q, core, rows_of, p] for core in (0, 1) for q in range(4)], axis=0)
        part_src[p, rows_of] = dot(comb_w[p, rows_of], rows).astype(BF)

    for step, rows_of in ((0, ONE), (1, TWO)):
        results_in(step)
        for p in (3, 1, 2):
            weigh(p, rows_of)
            remote(
                part_src.at[p, rows_of], part_rcv.at[c, p], p_s.at[rows_of * 3 + p - 1], p_r.at[c * 3 + p - 1],
                first(4 - DIST[p], rows_of),
            )
    weigh(0, ONE)
    results_in(2)
    weigh(0, TWO)
    remote(part_src.at[0, other], part_rcv.at[c, 0], p_s.at[6], p_r.at[6], dev(0, 0, other))
    part_rcv[c, 0] = part_src[0, c]
    for cp in sends[:before]:
        cp.wait_send()

    @pl.when(has_w)
    def _():
        for cp in w_cp:
            cp.wait_send()

    relays[0][1].wait_send()

    arrived(hfin.at[other], h_r.at[2])
    arrived(part_rcv.at[other, 0], p_r.at[6])
    values = []
    total = jnp.zeros((128, 1), F32)
    for half in (0, 1):
        v = hfin[half].astype(F32) + part_rcv[half, 0].astype(F32)
        for p in (1, 2, 3):
            arrived(part_rcv.at[half, p], p_r.at[half * 3 + p - 1])
            v = v + part_rcv[half, p].astype(F32)
        total = total + jnp.sum(v * v, axis=1, keepdims=True)
        values.append(v)
    scale = lax.rsqrt(total * (1.0 / 1024.0) + 1e-06)
    for half in (0, 1):
        cols = slice(half * 512, half * 512 + 512)
        out_ref[:, cols] = (values[half] * scale * post[:, cols]).astype(BF)
    for cp in sends[before:]:
        cp.wait_send()


def on_device(
    attention, residual, out_proj, pre_gain, post_gain, slot_gate_up, slot_down, expert_ids, copy_choice,
    placement, request_age, decode_flag, capacity, route_weight,
):
    dma = pltpu.SemaphoreType.DMA
    vm = pltpu.VMEM
    done = pl.pallas_call(
        kernel,
        out_shape=jax.ShapeDtypeStruct((128, 1024), BF),
        in_specs=[pl.BlockSpec(memory_space=pl.ANY)] * 14,
        out_specs=pl.BlockSpec(memory_space=pltpu.VMEM),
        scratch_shapes=[
            vm((2, 1, 512), F32), vm((1, 1024), F32), vm((1024, 1024), BF), vm((512, 1024), BF),
            vm((8, 128), jnp.int32), vm((8, 128), jnp.int32), vm((1, 32), jnp.int32),
            vm((1, 128), jnp.int32), vm((1, 128), jnp.int32), vm((4, 32), jnp.int32), vm((8, 128), F32),
            vm((3, 2, 128, 1024), BF), vm((3, 2, 128, 512), BF), vm((2, 2, 512, 256), BF),
            vm((4, 2, 128, 512), BF), vm((2, 128, 512), BF),
            vm((2, 4, 32, 256), BF), vm((4, 2, 32, 256), BF),
            vm((4, 2, 256, 128), BF), vm((4, 2, 128, 256), BF),
            vm((8, 128), F32), vm((4, 8, 128), F32),
            vm((2, 4, 2, 4, 32, 512), BF), vm((2, 4, 2, 4, 32, 512), BF),
            vm((2, 4, 2, 4, 32, 512), BF), vm((4, 2, 2, 4, 32, 512), BF),
            vm((4, 2, 128, 512), BF), vm((2, 4, 128, 512), BF),
            dma((14,)), dma((6,)),
            dma((4,)), dma((1,)), dma((2, 2)),
            dma((5,)), dma((3, 2)), dma((5,)), dma((3, 2)),
            dma((7,)), dma((4, 2)),
            dma((3,)), dma((3,)), dma((4,)), dma((4,)),
            dma((3, 7)), dma((3, 7)), dma((3, 7)), dma((3, 7)), dma((7,)), dma((7,)),
        ],
        compiler_params=pltpu.CompilerParams(
            collective_id=0, has_side_effects=True, vmem_limit_bytes=67_000_000
        ),
        cost_estimate=pl.CostEstimate(flops=5_000_000_000, bytes_accessed=5_000_000, transcendentals=600_000),
        name="moe_layer",
    )(
        attention, residual, out_proj.reshape(2, 512, 256), pre_gain.reshape(2, 1, 512), post_gain.reshape(1, -1),
        slot_gate_up[0], slot_down[0], expert_ids.T, copy_choice.T, placement.reshape(1, -1),
        request_age.reshape(1, -1), decode_flag.reshape(1, -1), capacity, route_weight.T,
    )
    return done


def solution(mesh):
    rows = P(("grp", "ep"), None)
    placed = (
        rows, rows, P(None, "grp"), P(), P(), P("ep", None, None), P("ep", None, None), rows, rows, P(),
        P(("grp", "ep")), P(("grp", "ep")), P(), rows,
    )
    return jax.shard_map(on_device, mesh=mesh, in_specs=placed, out_specs=rows, check_vma=False)
```

```python
import jax
import jax.numpy as jnp
from jax import lax
from jax.experimental import pallas as pl
from jax.experimental.pallas import tpu as pltpu
from jax.sharding import PartitionSpec as P

MESH = pl.DeviceIdType.MESH
BF = jnp.bfloat16
F32 = jnp.float32
DIST = (0, 1, 3, 2)
ONE, TWO = 1, 0


def dot(a, b):
    return jnp.dot(a, b, preferred_element_type=F32)


def kernel(
    att_h, res_h, wo_h, pre_h, post_h, gu_h, dn_h, ids_h, cc_h, place_h, age_h, flag_h, cap_h, rw_h,
    out_ref,
    pre, post, gu, dn, ids, cc, place, age, flag, cap, rw,
    att, res, wmine, hall, hfin, mw_src, mw_all, sel, comb_w, ss_src, ss_rcv,
    comp, rec, ob, comb, part_src, part_rcv,
    in_sem, loc_sem, w_s, w_f, w_r, a_s, a_r, r_s, r_r, m_s, m_r, h_s, h_r, q_s, q_r, d_s, d_r, e_s, e_r, p_s, p_r,
):
    z = lax.axis_index("grp")
    e = lax.axis_index("ep")
    x, y, c = e >> 3, (e >> 1) & 3, e & 1
    other = 1 - c

    def dev(dx, dy, core):
        return (z, ((x + dx) & 3) * 8 + ((y + dy) & 3) * 2 + core)

    def first(d, core):
        return dev(d * other, d * c, core)

    def second(d, core):
        return dev(d * c, d * other, core)

    bar = pltpu.get_barrier_semaphore()
    up, down = ((z + 1) & 3, e), ((z + 3) & 3, e)
    greet = [up, down, dev(0, 0, other)]
    for d in (1, 2, 3):
        greet += [first(d, 0), first(d, 1), second(d, c)]
    for to in greet:
        pl.semaphore_signal(bar, inc=1, device_id=to, device_id_type=MESH)

    def half_of(half):
        return pl.ds(pl.multiple_of(half * 512, 512), 512)

    sends = []

    def remote(src, dst, ss, rs, to):
        cp = pltpu.make_async_remote_copy(
            src_ref=src, dst_ref=dst, send_sem=ss, recv_sem=rs, device_id=to, device_id_type=MESH
        )
        cp.start()
        sends.append(cp)

    def arrived(dst, rs):
        pltpu.make_async_remote_copy(
            src_ref=dst, dst_ref=dst, send_sem=rs, recv_sem=rs, device_id=dev(0, 0, other), device_id_type=MESH
        ).wait_recv()

    has_w = c == z >> 1
    mine = z & 1
    w_cp = []
    for i, (to, h) in enumerate(((up, 0), (down, 1), (up, 1), (down, 0))):
        w_cp.append(
            pltpu.make_async_remote_copy(
                src_ref=wo_h.at[h], dst_ref=wmine.at[mine, h], send_sem=w_s.at[i], recv_sem=w_r.at[mine, h],
                device_id=to, device_id_type=MESH,
            )
        )
    w_local = pltpu.make_async_copy(wo_h, wmine.at[mine], in_sem.at[13])
    turn = (z - 2 * c) & 3
    near = ((turn + 1) >> 1) & 1
    relays = []
    for t, q, h, to in ((0, 1, 1, down), (1, 0, 0, up), (2, 1, 0, up), (3, 0, 1, down)):
        relays.append(
            (
                t,
                pltpu.make_async_remote_copy(
                    src_ref=wmine.at[q, h], dst_ref=wmine.at[q, h], send_sem=w_f.at[0], recv_sem=w_r.at[q, h],
                    device_id=to, device_id_type=MESH,
                ),
            )
        )
    pl.semaphore_wait(bar, len(greet))

    @pl.when(has_w)
    def _():
        for cp in w_cp:
            cp.start()
        w_local.start()

    k = 0
    for p in (1, 2):
        d = DIST[p]
        for half, to in ((0, dev(d, 0, 0)), (1, dev(0, d, 1))):
            remote(att_h, att.at[p, c], a_s.at[k], a_r.at[p, c], to)
            remote(res_h.at[:, half * 512 : half * 512 + 512], res.at[p, c], r_s.at[k], r_r.at[p, c], to)
            k += 1
    remote(att_h, att.at[0, c], a_s.at[k], a_r.at[0, c], dev(0, 0, other))
    remote(res_h.at[:, half_of(other)], res.at[0, c], r_s.at[k], r_r.at[0, c], dev(0, 0, other))

    loads = []
    for i, (src, dst) in enumerate(
        (
            (ids_h, ids), (cc_h, cc), (place_h, place), (age_h, age), (flag_h, flag), (cap_h, cap), (rw_h, rw),
            (att_h, att.at[0, c]), (res_h.at[:, half_of(c)], res.at[0, c]), (pre_h, pre), (post_h, post),
            (gu_h, gu), (dn_h, dn),
        )
    ):
        cp = pltpu.make_async_copy(src, dst, in_sem.at[i])
        cp.start()
        loads.append(cp)

    for cp in loads[:7]:
        cp.wait()
    row = lax.broadcasted_iota(jnp.int32, (128, 128), 0)
    lane = lax.broadcasted_iota(jnp.int32, (128, 128), 1)
    eye = row == lane
    pr_row = (flag[...] * 1048576 + age[...]).astype(F32)
    pr_col = jnp.sum(jnp.where(eye, pr_row, 0.0), axis=1, keepdims=True)
    ahead = jnp.where((pr_col > pr_row) | ((pr_col == pr_row) & (row < lane)), 1.0, 0.0)
    t = lax.broadcasted_iota(jnp.int32, (128, 32), 0)
    slot_lane = lax.broadcasted_iota(jnp.int32, (128, 32), 1)
    copy_of = t % 4
    px, py = t // 32, (t // 4) % 4
    dx = jnp.where(px < 2, px, 5 - px)
    dy = jnp.where(py < 2, py, 5 - py)
    slot = (((x + dx) % 4) * 4 + (y + dy) % 4) * 2 + (t // 16) % 2
    here = slot_lane == slot
    expert = jnp.sum(jnp.where(here, place[...].astype(F32), 0.0), axis=1, keepdims=True)
    code_col = expert * 4.0 + copy_of[:, :1].astype(F32)
    capf = cap[...].astype(F32)
    cap_sel = jnp.zeros((128, 32), F32)
    for g in range(4):
        cap_sel = jnp.where(here & (copy_of == g), capf[g : g + 1, :], cap_sel)
    cap_col = jnp.sum(cap_sel, axis=1, keepdims=True)
    code = (ids[...] * 4 + cc[...]).astype(F32)
    hits = jnp.zeros((128, 128), F32)
    weight = jnp.zeros((128, 128), F32)
    for i in range(8):
        same = code_col == code[i : i + 1, :]
        hits = jnp.where(same, 1.0, hits)
        weight = jnp.where(same, rw[i : i + 1, :], weight)
    counts = dot(hits.astype(BF), ahead.astype(BF))
    place_in = jnp.where((hits > 0.5) & (counts < cap_col), counts, 99.0)
    pw = jnp.concatenate([place_in, weight], axis=1)
    for p in range(4):
        mw_src[0, p] = pw[p * 32 : p * 32 + 32].astype(BF)
        blocks = []
        for core in range(2):
            for q in range(4):
                lo = q * 32 + core * 16 + p * 4
                blocks.append(pw[lo : lo + 4])
        mw_src[1, p] = jnp.concatenate(blocks, axis=0).astype(BF)
    k = 0
    for p in (1, 2, 3):
        d = DIST[p]
        for half, to in ((0, dev(d, 0, 0)), (1, dev(0, d, 1))):
            remote(mw_src.at[half, p], mw_all.at[p, c], m_s.at[k], m_r.at[p, c], to)
            k += 1
    remote(mw_src.at[other, 0], mw_all.at[0, c], m_s.at[k], m_r.at[0, c], dev(0, 0, other))
    mw_all[0, c] = mw_src[c, 0]

    for t, cp in relays:

        @pl.when(turn == t)
        def _():
            cp.wait_recv()
            cp.start()

    grow = jnp.where(
        lax.broadcasted_iota(jnp.int32, (256, 32), 0) // 8 == lax.broadcasted_iota(jnp.int32, (256, 32), 1), 1.0, 0.0
    ).astype(BF)
    p_row = (lax.broadcasted_iota(jnp.int32, (256, 128), 0) % 8).astype(F32)
    p_lane = (lax.broadcasted_iota(jnp.int32, (128, 256), 1) % 8).astype(F32)
    arrived(mw_all.at[0, other], m_r.at[0, other])
    for p in range(4):
        for core in (0, 1):
            if p:
                arrived(mw_all.at[p, core], m_r.at[p, core])
            both = mw_all[p, core]
            sel[p, core] = jnp.where(dot(grow, both[:, :128]) == p_row, 1.0, 0.0).astype(BF)
            wide = lax.dot_general(both, grow, (((0,), (1,)), ((), ())), preferred_element_type=F32)
            comb_w[p, core] = jnp.where(wide[:128] == p_lane, wide[128:], 0.0).astype(BF)

    def quarter_in(q):
        @pl.when(has_w & (mine == q))
        def _():
            w_local.wait()

        for h in (0, 1):
            relayed = ((0, 1, 1), (1, 0, 0), (2, 1, 0), (3, 0, 1))
            done = [t for t, rq, rh in relayed if rq == q and rh == h]
            waits = ~(has_w & (mine == q))
            for t in done:
                waits = waits & (turn != t)

            @pl.when(waits)
            def _():
                arrived(wmine.at[q, h], w_r.at[q, h])

    def project(p, q):
        rows = att[p].reshape(256, 1024)
        part = dot(rows, wmine[q].reshape(1024, 256)).reshape(2, 128, 256)
        cols = pl.ds(pl.multiple_of(q * 256, 256), 256)
        hall[p, :, :, cols] = (res[p, :, :, cols].astype(F32) + part).astype(BF)

    def squares(p, core):
        wide = hall[p, core].astype(F32)
        return jnp.sum(wide * wide, axis=1, keepdims=True)

    for cp in loads[7:]:
        cp.wait()
    arrived(att.at[0, other], a_r.at[0, other])
    arrived(res.at[0, other], r_r.at[0, other])
    for p in (1, 2):
        for core in (0, 1):
            arrived(att.at[p, core], a_r.at[p, core])
            arrived(res.at[p, core], r_r.at[p, core])
    for q in (0, 1):

        @pl.when(near == q)
        def _():
            quarter_in(q)

    for p in range(3):
        project(p, near)
    for q in (0, 1):

        @pl.when(near != q)
        def _():
            quarter_in(q)

    project(0, 1 - near)
    own_ss = {}
    for core in (0, 1):
        own_ss[0, core] = squares(0, core)
        ss_src[core : core + 1, :] = jnp.sum(jnp.where(eye, own_ss[0, core], 0.0), axis=0, keepdims=True)
    for p in (1, 2, 3):
        remote(ss_src, ss_rcv.at[p], q_s.at[p], q_r.at[p], second(DIST[p], other))
    remote(ss_src, ss_rcv.at[0], q_s.at[0], q_r.at[0], dev(0, 0, other))
    project(1, 1 - near)
    remote(hall.at[1, 0], hall.at[3, 0], h_s.at[0], h_r.at[0], first(1, c))
    project(2, 1 - near)
    remote(hall.at[2, 1], hall.at[3, 1], h_s.at[1], h_r.at[1], first(3, c))
    for p in (1, 2):
        for core in (0, 1):
            own_ss[p, core] = squares(p, core)
    gain = pre[c]

    def compact(p, core):
        own = own_ss[p, core]
        total = own + jnp.sum(jnp.where(eye, ss_rcv[p, core : core + 1, :], 0.0), axis=1, keepdims=True)
        scale = lax.rsqrt(total * (1.0 / 1024.0) + 1e-06)
        normed = (hall[p, core].astype(F32) * scale * gain).astype(BF)
        return dot(sel[p, core], normed).astype(BF).reshape(2, 4, 32, 512)

    local = []

    def part_of(kind):
        return ((ONE, pl.ds(0, 3)), (ONE, 3), (TWO,))[kind]

    def spread(kind):
        for p in (3, 1, 2):
            for core in (0, 1):
                remote(
                    comp.at[(core, p) + part_of(kind)], rec.at[(c, p) + part_of(kind)],
                    d_s.at[kind, core * 3 + p - 1], d_r.at[kind, c * 3 + p - 1], second(DIST[p], core),
                )
        remote(
            comp.at[(other, 0) + part_of(kind)], rec.at[(c, 0) + part_of(kind)], d_s.at[kind, 6], d_r.at[kind, 6],
            dev(0, 0, other),
        )
        cp = pltpu.make_async_copy(
            comp.at[(c, 0) + part_of(kind)], rec.at[(c, 0) + part_of(kind)], loc_sem.at[kind]
        )
        cp.start()
        local.append(cp)

    for p in range(3):
        arrived(ss_rcv.at[p], q_r.at[p])
        comp[:, :, ONE, p] = compact(p, ONE)
    spread(0)
    arrived(ss_rcv.at[3], q_r.at[3])
    for core in (0, 1):
        arrived(hall.at[3, core], h_r.at[core])
        own_ss[3, core] = squares(3, core)
    comp[:, :, ONE, 3] = compact(3, ONE)

    spread(1)
    for p in range(4):
        comp[:, :, TWO, p] = compact(p, TWO)
    spread(2)
    remote(hall.at[0, other], hfin.at[c], h_s.at[2], h_r.at[2], dev(0, 0, other))
    hfin[c] = hall[0, c]

    def places_in(kind):
        for half in (0, 1):
            for p in (1, 2, 3):
                arrived(rec.at[(half, p) + part_of(kind)], d_r.at[kind, half * 3 + p - 1])
        arrived(rec.at[(other, 0) + part_of(kind)], d_r.at[kind, 6])
        local[kind].wait()

    def back_part(kind):
        return ((ONE,), (TWO, pl.ds(1, 3)), (TWO, 0))[kind]

    back = []

    def give_back(kind, half, p):
        d = 4 - DIST[p]
        remote(
            ob.at[(half, p) + back_part(kind)], comb.at[(p, c) + back_part(kind)], e_s.at[kind, half * 3 + p - 1],
            e_r.at[kind, c * 3 + p - 1], dev(0, d, 0) if half == 0 else dev(d, 0, 1),
        )

    def give_chip(kind):
        remote(
            ob.at[(other, 0) + back_part(kind)], comb.at[(0, c) + back_part(kind)], e_s.at[kind, 6], e_r.at[kind, 6],
            dev(0, 0, other),
        )
        cp = pltpu.make_async_copy(
            ob.at[(c, 0) + back_part(kind)], comb.at[(0, c) + back_part(kind)], loc_sem.at[3 + kind]
        )
        cp.start()
        back.append(cp)

    for step, rows_of in ((0, ONE), (1, TWO)):
        if step == 0:
            places_in(0)
            places_in(1)
        else:
            places_in(2)

        for pair in (1, 0):
            blocks = [(qy, qx) for qy in (2 * pair, 2 * pair + 1) for qx in range(4)]
            xa = jnp.concatenate([rec[0, qy, rows_of, qx] for qy, qx in blocks], axis=0)
            xb = jnp.concatenate([rec[1, qx, rows_of, qy] for qy, qx in blocks], axis=0)
            gate = dot(xa, gu[:512, :512]) + dot(xb, gu[512:, :512])
            raised = dot(xa, gu[:512, 512:]) + dot(xb, gu[512:, 512:])
            inner = (gate / (1.0 + jnp.exp(-gate)) * raised).astype(BF)
            made = dot(inner, dn[...]).astype(BF)
            for i, (qy, qx) in enumerate(blocks):
                ob[0, qy, rows_of, qx] = made[i * 32 : i * 32 + 32, :512]
                ob[1, qx, rows_of, qy] = made[i * 32 : i * 32 + 32, 512:]
            if pair == 1:
                early = ((0, 3), (0, 2))
            else:
                early = ((1, 3), (1, 1), (0, 1), (1, 2))
            for half, p in early:
                give_back(step, half, p)
        give_chip(step)
    for p in (3, 1, 2):
        for half in (0, 1):
            give_back(2, half, p)
    give_chip(2)

    before = len(sends)

    def results_in(kind):
        for core in (0, 1):
            for p in (1, 2, 3):
                arrived(comb.at[(p, core) + back_part(kind)], e_r.at[kind, core * 3 + p - 1])
        arrived(comb.at[(0, other) + back_part(kind)], e_r.at[kind, 6])
        back[kind].wait()

    def weigh(p, rows_of):
        rows = jnp.concatenate([comb[q, core, rows_of, p] for core in (0, 1) for q in range(4)], axis=0)
        part_src[p, rows_of] = dot(comb_w[p, rows_of], rows).astype(BF)

    for step, rows_of in ((0, ONE), (1, TWO)):
        results_in(step)
        for p in (3, 1, 2):
            weigh(p, rows_of)
            remote(
                part_src.at[p, rows_of], part_rcv.at[c, p], p_s.at[rows_of * 3 + p - 1], p_r.at[c * 3 + p - 1],
                first(4 - DIST[p], rows_of),
            )
    weigh(0, ONE)
    results_in(2)
    weigh(0, TWO)
    remote(part_src.at[0, other], part_rcv.at[c, 0], p_s.at[6], p_r.at[6], dev(0, 0, other))
    part_rcv[c, 0] = part_src[0, c]
    for cp in sends[:before]:
        cp.wait_send()

    @pl.when(has_w)
    def _():
        for cp in w_cp:
            cp.wait_send()

    relays[0][1].wait_send()

    arrived(hfin.at[other], h_r.at[2])
    arrived(part_rcv.at[other, 0], p_r.at[6])
    values = []
    total = jnp.zeros((128, 1), F32)
    for half in (0, 1):
        v = hfin[half].astype(F32) + part_rcv[half, 0].astype(F32)
        for p in (1, 2, 3):
            arrived(part_rcv.at[half, p], p_r.at[half * 3 + p - 1])
            v = v + part_rcv[half, p].astype(F32)
        total = total + jnp.sum(v * v, axis=1, keepdims=True)
        values.append(v)
    scale = lax.rsqrt(total * (1.0 / 1024.0) + 1e-06)
    for half in (0, 1):
        cols = slice(half * 512, half * 512 + 512)
        out_ref[:, cols] = (values[half] * scale * post[:, cols]).astype(BF)
    for cp in sends[before:]:
        cp.wait_send()


def on_device(
    attention, residual, out_proj, pre_gain, post_gain, slot_gate_up, slot_down, expert_ids, copy_choice,
    placement, request_age, decode_flag, capacity, route_weight,
):
    dma = pltpu.SemaphoreType.DMA
    vm = pltpu.VMEM
    done = pl.pallas_call(
        kernel,
        out_shape=jax.ShapeDtypeStruct((128, 1024), BF),
        in_specs=[pl.BlockSpec(memory_space=pl.ANY)] * 14,
        out_specs=pl.BlockSpec(memory_space=pltpu.VMEM),
        scratch_shapes=[
            vm((2, 1, 512), F32), vm((1, 1024), F32), vm((1024, 1024), BF), vm((512, 1024), BF),
            vm((8, 128), jnp.int32), vm((8, 128), jnp.int32), vm((1, 32), jnp.int32),
            vm((1, 128), jnp.int32), vm((1, 128), jnp.int32), vm((4, 32), jnp.int32), vm((8, 128), F32),
            vm((3, 2, 128, 1024), BF), vm((3, 2, 128, 512), BF), vm((2, 2, 512, 256), BF),
            vm((4, 2, 128, 512), BF), vm((2, 128, 512), BF),
            vm((2, 4, 32, 256), BF), vm((4, 2, 32, 256), BF),
            vm((4, 2, 256, 128), BF), vm((4, 2, 128, 256), BF),
            vm((8, 128), F32), vm((4, 8, 128), F32),
            vm((2, 4, 2, 4, 32, 512), BF), vm((2, 4, 2, 4, 32, 512), BF),
            vm((2, 4, 2, 4, 32, 512), BF), vm((4, 2, 2, 4, 32, 512), BF),
            vm((4, 2, 128, 512), BF), vm((2, 4, 128, 512), BF),
            dma((14,)), dma((6,)),
            dma((4,)), dma((1,)), dma((2, 2)),
            dma((5,)), dma((3, 2)), dma((5,)), dma((3, 2)),
            dma((7,)), dma((4, 2)),
            dma((3,)), dma((3,)), dma((4,)), dma((4,)),
            dma((3, 7)), dma((3, 7)), dma((3, 7)), dma((3, 7)), dma((7,)), dma((7,)),
        ],
        compiler_params=pltpu.CompilerParams(
            collective_id=0, has_side_effects=True, vmem_limit_bytes=67_000_000
        ),
        cost_estimate=pl.CostEstimate(flops=5_000_000_000, bytes_accessed=5_000_000, transcendentals=600_000),
        name="moe_layer",
    )(
        attention, residual, out_proj.reshape(2, 512, 256), pre_gain.reshape(2, 1, 512), post_gain.reshape(1, -1),
        slot_gate_up[0], slot_down[0], expert_ids.T, copy_choice.T, placement.reshape(1, -1),
        request_age.reshape(1, -1), decode_flag.reshape(1, -1), capacity, route_weight.T,
    )
    return done


def solution(mesh):
    rows = P(("grp", "ep"), None)
    placed = (
        rows, rows, P(None, "grp"), P(), P(), P("ep", None, None), P("ep", None, None), rows, rows, P(),
        P(("grp", "ep")), P(("grp", "ep")), P(), rows,
    )
    return jax.shard_map(on_device, mesh=mesh, in_specs=placed, out_specs=rows, check_vma=False)
```
